256 devices in a mesh: term: 16 (over z_lo, x), space: 16 (over y, z_hi, core).
Axes of the slice: x: 4, y: 4, z: 8 (z_hi: 2, z_lo: 4; z = z_hi * 4 + z_lo), core: 2. Of those that a mesh axis runs over, the one named last changes fastest.
Arguments:
- fields: float32 [288, 512, 256], P('term', 'space'), may hold values from -6 to 6
- modes: float32 [11, 512, 256], P(None, 'space'), may hold values from -6 to 6
- pair_list: int32 [2048, 3], replicated, may hold values from 0 to 287, as said below
- pair_value: float32 [2048], replicated, may hold values from -2 to 2
- assign: int32 [288], replicated, may hold values from 0 to 287, each once
Outputs:
- result: float32 [288, 512, 256], P('term', 'space')
The draws below stay inside these ranges and needn't reach their ends.
Inputs may be any that keep to these rules, and one draw needn't show every extreme that they name: `pair_list`: terms are the multi-indices of total degree 3 or less over 11 - 1 variables in graded order, the first 288 of them, terms beyond the 286 such indices having none. Every term t has a row (t, t, 0); for each term alpha and variable v whose index alpha + e_v is also a term u there are rows (alpha, u, v + 1) and (u, alpha, v + 1); these rows stand once each, and the remaining rows repeat diagonal rows (t, t, 0). Rows are in random order.
All inputs are finite; a program needn't handle non-finite values.
Results may differ from the reference program's by a relative error of at most 0.00012.
Values sent between devices are 32-bit elements; how exact they have to be, the bound alone decides.
No kernel may reach another device: no remote copies, remote signals or barrier semaphores. Data moves between devices by JAX's collectives and lax.ppermute only.
A program may use at most 64 MiB of HBM per device.

```python
import jax
import jax.numpy as jnp
import numpy as np
from jax import lax

K = 11
P_SIZE = 288
CY = 256
NPAIR = 2048
NX = 512


def compositions(amount_left, places):
    if places == 1:
        return [(amount_left,)]
    output_list = []
    for first_part in range(amount_left, -1, -1):
        for remainder in compositions(amount_left - first_part, places - 1):
            output_list.append((first_part,) + remainder)
    return output_list


def coupling_rows(term_count, variables):
    indices_list = []
    for degree_now in range(4):
        indices_list.extend(compositions(degree_now, variables))
    indices_list = indices_list[:term_count]
    lookup_table = {}
    for position, multi_index in enumerate(indices_list):
        lookup_table[multi_index] = position
    rows_list = []
    for position in range(term_count):
        rows_list.append((position, position, 0))
    for position, multi_index in enumerate(indices_list):
        for variable in range(variables):
            raised = list(multi_index)
            raised[variable] = raised[variable] + 1
            raised = tuple(raised)
            if raised in lookup_table:
                target = lookup_table[raised]
                rows_list.append((position, target, variable + 1))
                rows_list.append((target, position, variable + 1))
    return np.array(rows_list, dtype=np.int32).reshape(-1, 3)


def draw_pair_list(key, part):
    key = jax.random.fold_in(key, 7)
    fixed_rows = coupling_rows(P_SIZE, K - 1)
    extra_rows = NPAIR - fixed_rows.shape[0]
    first_key, second_key = jax.random.split(key)
    repeats = jax.random.randint(first_key, (extra_rows,), 0, P_SIZE).astype(jnp.int32)
    padding = jnp.stack([repeats, repeats, jnp.zeros_like(repeats)], axis=1)
    combined = jnp.concatenate([jnp.asarray(fixed_rows, jnp.int32), padding], axis=0)
    order = jax.random.permutation(second_key, NPAIR)
    return combined[order].astype(jnp.int32)


def steps_of(stream_key, dims, pieces, least, largest):
    def one(dim, parts):
        steps = jax.random.uniform(jax.random.fold_in(jax.random.fold_in(stream_key, 6), dim), (parts,), jnp.float32, least / len(pieces), largest / len(pieces))
        return jnp.repeat(jnp.exp(steps), dims[dim] // parts).reshape((-1,) + (1,) * (len(dims) - dim - 1))

    loudness = one(*pieces[0])
    for cut in pieces[1:]:
        loudness = loudness * one(*cut)
    return loudness


def normal_values(own_key, extent, deviation, limit, cuts=(), kind=jnp.bfloat16):
    entries = deviation * jax.random.normal(own_key, extent, jnp.float32)
    if cuts:
        entries = entries * steps_of(own_key, extent, cuts, -0.22, 0.18)
    return jnp.clip(entries, -limit, limit).astype(kind)


def setup_inputs(seed: int = 0) -> dict:
    splits = jax.random.split(jax.random.key(seed), 6)
    fields = normal_values(splits[0], (P_SIZE, NX, CY), 1.0, 6.0, ((0, 16), (1, 16)), jnp.float32)
    modes = normal_values(splits[1], (K, NX, CY), 1.0, 6.0, ((1, 16),), jnp.float32)
    pair_list = draw_pair_list(jax.random.fold_in(splits[5], 71), 0)
    pair_value = normal_values(splits[3], (NPAIR,), 0.3, 2.0, (), jnp.float32)
    assign = jax.random.permutation(splits[4], P_SIZE).astype(jnp.int32)
    return dict(fields=fields, modes=modes, pair_list=pair_list, pair_value=pair_value, assign=assign)


def diffuse(field, coef):
    centre = field[..., 1:-1, :]
    centre_coef = coef[..., 1:-1, :]
    widths = [(0, 0)] * (field.ndim - 1) + [(1, 1)]
    side_field = jnp.pad(centre, widths)
    side_coef = jnp.pad(centre_coef, [(0, 0)] * (centre_coef.ndim - 1) + [(1, 1)])
    result = 0.5 * (centre_coef + coef[..., :-2, :]) * (centre - field[..., :-2, :])
    result = result + 0.5 * (centre_coef + coef[..., 2:, :]) * (centre - field[..., 2:, :])
    result = result + 0.5 * (centre_coef + side_coef[..., :-2]) * (centre - side_field[..., :-2])
    result = result + 0.5 * (centre_coef + side_coef[..., 2:]) * (centre - side_field[..., 2:])
    return result


def reference(fields, modes, pair_list, pair_value, assign):
    slot_of = jnp.zeros((P_SIZE,), jnp.int32).at[assign].set(jnp.arange(P_SIZE, dtype=jnp.int32))
    row_slot = slot_of[pair_list[:, 0]]
    col_slot = slot_of[pair_list[:, 1]]
    table = jnp.zeros((K, P_SIZE, P_SIZE), jnp.float32).at[pair_list[:, 2], row_slot, col_slot].add(pair_value)
    padded = jnp.pad(fields, ((0, 0), (1, 1), (0, 0)))
    padded_modes = jnp.pad(modes, ((0, 0), (1, 1), (0, 0)))

    def step(total, mode):
        applied = diffuse(padded, padded_modes[mode])
        flat = applied.reshape(P_SIZE, -1)
        summed = jnp.dot(table[mode], flat, precision=lax.Precision.HIGHEST, preferred_element_type=jnp.float32)
        return total + summed.reshape(total.shape), None

    start_total = jnp.zeros(fields.shape, jnp.float32)
    result, unused = lax.scan(step, start_total, jnp.arange(K, dtype=jnp.int32))
    return result
```

```python
import functools

import jax
import jax.numpy as jnp
from jax import lax
from jax.experimental import pallas as pl
from jax.experimental.pallas import tpu as pltpu
from jax.sharding import PartitionSpec as P

PAIRS = 9
ROWS = 96
TOP = 72
BOTTOM = 81
SIDE = 90
LOWER = 66
VARS = 10


def lanes_of(shape=(8, 128)):
    return lax.broadcasted_iota(jnp.int32, shape, 1)


def subs_of(shape=(8, 128)):
    return lax.broadcasted_iota(jnp.int32, shape, 0)


def pack_kernel(f_ref, out_ref):
    lane, sub = lanes_of(), subs_of()
    low = lane < 64
    even = lane % 2 == 0
    spare = lane % 64 >= 32
    for r in range(4):
        near, far = [], []
        for h in range(2):
            ga = jnp.zeros((8, 128), jnp.float32)
            gb = jnp.zeros((8, 128), jnp.float32)
            for p in range(PAIRS):
                a = f_ref[p, pl.ds(8 * r, 8), pl.ds(128 * h, 128)]
                b = f_ref[p + PAIRS, pl.ds(8 * r, 8), pl.ds(128 * h, 128)]
                both = (
                    jnp.where(low, a, pltpu.roll(b, 64, 1)),
                    jnp.where(low, pltpu.roll(a, 64, 1), b),
                )
                for o in range(2):
                    c = 2 * h + o
                    out_ref[4 * r + c, pl.ds(8 * p, 8), :] = both[o]
                    if r < 3:
                        out_ref[4 * (r + 1) + c, pl.ds(TOP + p, 1), :] = both[o][7:8]
                    if r > 0:
                        out_ref[4 * (r - 1) + c, pl.ds(BOTTOM + p, 1), :] = both[o][0:1]
                here = (lane % 64) // 2 == p
                ga = jnp.where(here, pltpu.roll(a, (2 * p - 63) % 128, 1), ga)
                gb = jnp.where(here, pltpu.roll(b, 2 * p + 1, 1), gb)
            near.append(jnp.where(low, ga, gb))
            far.append(pltpu.roll(jnp.where(low, gb, ga), 64, 1))
        zero = jnp.zeros((8, 128), jnp.float32)
        sides = (
            jnp.where(even, zero, near[0]),
            jnp.where(even, near[0], far[1]),
            jnp.where(even, far[0], near[1]),
            jnp.where(even, near[1], zero),
        )
        for c in range(4):
            moved = pltpu.roll(pltpu.roll(sides[c], 32, 1), 2, 0)
            kept = jnp.where(spare, moved, sides[c])
            out_ref[4 * r + c, pl.ds(SIDE, 6), :] = kept[0:6]


def edge_kernel(place_ref, sent_ref, above_ref, below_ref, modes_ref, out_ref, coef_ref):
    lane, sub = lanes_of(), subs_of()
    low = lane < 64
    low9 = lanes_of((PAIRS, 128)) < 64
    out_ref[...] = sent_ref[...]

    def place(ref, row):
        for h in range(2):
            a = ref[pl.ds(0, PAIRS), pl.ds(128 * h, 128)]
            b = ref[pl.ds(PAIRS, PAIRS), pl.ds(128 * h, 128)]
            out_ref[2 * h, pl.ds(row, PAIRS), :] = jnp.where(low9, a, pltpu.roll(b, 64, 1))
            out_ref[2 * h + 1, pl.ds(row, PAIRS), :] = jnp.where(low9, pltpu.roll(a, 64, 1), b)

    @pl.when(pl.program_id(0) == 0)
    def _():
        place(above_ref, 0)
        block_row = place_ref[0] // 4
        block_col = place_ref[0] % 4
        first = block_row == 0
        last = block_row == 3
        odd = block_col % 2 == 1
        right_half = block_col >= 2
        wide_lane = lanes_of((8, 256))
        wide_sub = subs_of((8, 256))
        count = modes_ref.shape[0]

        def one(k, carry):
            here = modes_ref[k, pl.ds(pl.multiple_of(8 * block_row, 8), 8), :]
            before = modes_ref[k, pl.ds(pl.multiple_of(8 * jnp.maximum(block_row - 1, 0), 8), 8), :]
            after = modes_ref[k, pl.ds(pl.multiple_of(8 * jnp.minimum(block_row + 1, 3), 8), 8), :]
            over = jnp.where(first, above_ref[pl.ds(2 * PAIRS + k, 1), :], before[7:8])
            under = jnp.where(last, below_ref[pl.ds(2 * PAIRS + k, 1), :], after[0:1])
            up = jnp.where(wide_sub == 0, over, pltpu.roll(here, 1, 0))
            down = jnp.where(wide_sub == 7, under, pltpu.roll(here, 7, 0))
            left = jnp.where(wide_lane == 0, 0.0, pltpu.roll(here, 1, 1))
            right = jnp.where(wide_lane == 255, 0.0, pltpu.roll(here, 255, 1))

            def both(x, y):
                x = 0.5 * (here + x)
                y = 0.5 * (here + y)
                x = jnp.where(right_half, x[:, 128:], x[:, :128])
                y = jnp.where(right_half, y[:, 128:], y[:, :128])
                return jnp.where(
                    odd,
                    jnp.where(low, pltpu.roll(x, 64, 1), y),
                    jnp.where(low, x, pltpu.roll(y, 64, 1)),
                )

            coef_ref[k, pl.ds(0, 8), :] = both(up, down)
            coef_ref[k, pl.ds(8, 8), :] = both(left, right)
            return carry

        lax.fori_loop(0, count, one, 0)

    @pl.when(pl.program_id(0) == 1)
    def _():
        place(below_ref, PAIRS)


def mix_kernel(assign_ref, upper_ref, weight_ref, got_ref, coef_ref, out_ref, diff, total):
    lane, sub = lanes_of(), subs_of()
    low = lane < 64

    def load(group, carry):
        tail = got_ref[group, pl.ds(ROWS - 8, 8), :]
        beside = jnp.where(
            sub < 6, pltpu.roll(tail, 6, 0), pltpu.roll(pltpu.roll(tail, 96, 1), 4, 0)
        )
        coef_v = coef_ref[0, pl.ds(0, 8), :]
        coef_h = coef_ref[0, pl.ds(8, 8), :]
        for p in range(PAIRS):
            here = got_ref[group, pl.ds(8 * p, 8), :]
            up = jnp.where(sub == 0, got_ref[group, pl.ds(TOP + p, 1), :], pltpu.roll(here, 1, 0))
            down = jnp.where(sub == 7, got_ref[group, pl.ds(BOTTOM + p, 1), :], pltpu.roll(here, 7, 0))
            left = jnp.where(
                lane % 64 == 0, pltpu.roll(beside, (128 - 2 * p) % 128, 1), pltpu.roll(here, 1, 1)
            )
            right = jnp.where(
                lane % 64 == 63, pltpu.roll(beside, 62 - 2 * p, 1), pltpu.roll(here, 127, 1)
            )
            up, down, left, right = here - up, here - down, here - left, here - right
            for o in range(2):
                term = assign_ref[group * (2 * PAIRS) + o * PAIRS + p]
                if o == 0:
                    vert = jnp.where(low, up, pltpu.roll(down, 64, 1))
                    hori = jnp.where(low, left, pltpu.roll(right, 64, 1))
                else:
                    vert = jnp.where(low, pltpu.roll(up, 64, 1), down)
                    hori = jnp.where(low, pltpu.roll(left, 64, 1), right)
                diff[term, pl.ds(0, 8), :] = vert
                diff[term, pl.ds(8, 8), :] = hori
                total[term] = weight_ref[0, term] * (coef_v * vert + coef_h * hori)
        return carry

    lax.fori_loop(0, got_ref.shape[0], load, 0)

    def couple(term, carry):
        vert = diff[term, pl.ds(0, 8), :]
        hori = diff[term, pl.ds(8, 8), :]
        own = total[term]
        uppers = [upper_ref[v, term] for v in range(VARS)]
        sums = [total[upper] for upper in uppers]
        for v in range(VARS):
            coef_v = coef_ref[v + 1, pl.ds(0, 8), :]
            coef_h = coef_ref[v + 1, pl.ds(8, 8), :]
            upper = uppers[v]
            own = own + weight_ref[1 + v, term] * (
                coef_v * diff[upper, pl.ds(0, 8), :] + coef_h * diff[upper, pl.ds(8, 8), :]
            )
            sums[v] = sums[v] + weight_ref[1 + VARS + v, term] * (coef_v * vert + coef_h * hori)
        total[term] = own
        for v in range(VARS):
            total[uppers[v]] = sums[v]
        return carry

    lax.fori_loop(0, LOWER, couple, 0)

    def store(group, carry):
        for p in range(PAIRS):
            a = total[assign_ref[group * (2 * PAIRS) + p]]
            b = total[assign_ref[group * (2 * PAIRS) + PAIRS + p]]
            out_ref[group, pl.ds(8 * p, 8), :] = jnp.where(
                low, a + pltpu.roll(a, 64, 1), b + pltpu.roll(b, 64, 1)
            )
        return carry

    lax.fori_loop(0, got_ref.shape[0], store, 0)


def unpack_kernel(got_ref, out_ref):
    low = lanes_of() < 64
    for r in range(4):
        for h in range(2):
            for p in range(PAIRS):
                one = got_ref[4 * r + 2 * h, pl.ds(8 * p, 8), :]
                two = got_ref[4 * r + 2 * h + 1, pl.ds(8 * p, 8), :]
                out_ref[p, pl.ds(8 * r, 8), pl.ds(128 * h, 128)] = jnp.where(
                    low, one, pltpu.roll(two, 64, 1)
                )
                out_ref[p + PAIRS, pl.ds(8 * r, 8), pl.ds(128 * h, 128)] = jnp.where(
                    low, pltpu.roll(one, 64, 1), two
                )


def vmem():
    return pl.BlockSpec(memory_space=pltpu.VMEM)


def smem():
    return pl.BlockSpec(memory_space=pltpu.SMEM)


def f32(*shape):
    return jax.ShapeDtypeStruct(shape, jnp.float32)


PARAMS = pltpu.CompilerParams(vmem_limit_bytes=32 * 1024 * 1024)


def pack(fields, groups):
    return pl.pallas_call(
        pack_kernel,
        out_shape=f32(groups, ROWS, 128),
        in_specs=[vmem()],
        out_specs=vmem(),
        compiler_params=PARAMS,
        cost_estimate=pl.CostEstimate(flops=10**6, bytes_accessed=1400000, transcendentals=0),
    )(fields)


def edges(place, sent, above, below, modes):
    count = modes.shape[0]
    part = pl.BlockSpec((4, 24, 128), lambda i: (3 * i, 3, 0))
    whole = lambda x: pl.BlockSpec(x.shape, lambda i: (0,) * x.ndim)
    return pl.pallas_call(
        edge_kernel,
        grid=(2,),
        out_shape=(f32(*sent.shape), f32(count, 16, 128)),
        in_specs=[smem(), part, whole(above), whole(below), whole(modes)],
        out_specs=(part, pl.BlockSpec((count, 16, 128), lambda i: (0, 0, 0))),
        input_output_aliases={1: 0},
        compiler_params=PARAMS,
    )(place, sent, above, below, modes)


def mix(assign, uppers, weights, got, coef):
    groups = got.shape[0]
    return pl.pallas_call(
        mix_kernel,
        out_shape=f32(groups, 8 * PAIRS, 128),
        in_specs=[smem(), smem(), smem(), vmem(), vmem()],
        out_specs=vmem(),
        scratch_shapes=[
            pltpu.VMEM((groups * 2 * PAIRS, 16, 128), jnp.float32),
            pltpu.VMEM((groups * 2 * PAIRS, 8, 128), jnp.float32),
        ],
        compiler_params=PARAMS,
    )(assign, uppers, weights, got, coef)


def unpack(got, shape):
    return pl.pallas_call(
        unpack_kernel,
        out_shape=f32(*shape),
        in_specs=[vmem()],
        out_specs=vmem(),
        compiler_params=PARAMS,
    )(got)


def tables(pair_list, pair_value, terms, mode_count):
    row, col, mode = pair_list[:, 0], pair_list[:, 1], pair_list[:, 2]
    at = (jnp.minimum(row, col)[:, None] == jnp.arange(terms, dtype=jnp.int32)[None, :]).astype(jnp.float32)
    kinds = jnp.arange(1 + 3 * VARS, dtype=jnp.int32)[:, None]
    wanted = jnp.where(kinds <= VARS, kinds, (kinds - 1) % VARS + 1)
    side = jnp.where(
        kinds <= VARS, row <= col, jnp.where(kinds <= 2 * VARS, row > col, row < col)
    )
    value = jnp.where(kinds <= 2 * VARS, pair_value, col.astype(jnp.float32))
    value = jnp.where((mode[None, :] == wanted) & side, value, 0.0)
    found = jnp.dot(value, at, precision=lax.Precision.HIGHEST, preferred_element_type=jnp.float32)
    uppers = jnp.round(found[1 + 2 * VARS :]).astype(jnp.int32)
    return found[: 1 + 2 * VARS], uppers


def shards(fields, modes, pair_list, pair_value, assign):
    groups = lax.axis_size("term")
    count = lax.axis_size("space")
    ends = count - 1
    last = fields.shape[1] - 1
    head = jnp.concatenate([fields[:, 0], modes[:, 0]], axis=0)
    tail = jnp.concatenate([fields[:, last], modes[:, last]], axis=0)
    above = lax.ppermute(tail, "space", [(i, i + 1) for i in range(ends)])
    below = lax.ppermute(head, "space", [(i + 1, i) for i in range(ends)])
    weights, uppers = tables(pair_list, pair_value, groups * fields.shape[0], modes.shape[0])
    sent = pack(fields, groups)
    place = lax.axis_index("term").astype(jnp.int32).reshape(1)
    sent, coef = edges(place, sent, above, below, modes)
    got = lax.all_to_all(sent, "term", 0, 0, tiled=True)
    mixed = mix(assign, uppers, weights, got, coef)
    back = lax.all_to_all(mixed, "term", 0, 0, tiled=True)
    return unpack(back, fields.shape)


def solution(mesh):
    return jax.shard_map(
        shards,
        mesh=mesh,
        in_specs=(P("term", "space", None), P(None, "space", None), P(), P(), P()),
        out_specs=P("term", "space", None),
        check_vma=False,
    )
```

```python
import jax
import jax.numpy as jnp
from jax import lax
from jax.experimental import pallas as pl
from jax.experimental.pallas import tpu as pltpu
from jax.sharding import PartitionSpec as P

PAIRS = 9
BLOCK = 8 * PAIRS
ROWS = 96
FIRST = 72
SECOND = 81
SIDE = 90
LOWER = 66
VARS = 10


def holder(r, c):
    return 4 * c + (r ^ c)


def row_group(place):
    return (place & 3) ^ (place >> 2)


def lanes_of(shape=(8, 128)):
    return lax.broadcasted_iota(jnp.int32, shape, 1)


def subs_of(shape=(8, 128)):
    return lax.broadcasted_iota(jnp.int32, shape, 0)


def pack_kernel(f_ref, out_ref):
    lane = lanes_of()
    low = lane < 64
    even = lane % 2 == 0
    spare = lane % 64 >= 32
    for r in range(4):
        near, far = [], []
        for h in range(2):
            ga = jnp.zeros((8, 128), jnp.float32)
            gb = jnp.zeros((8, 128), jnp.float32)
            for p in range(PAIRS):
                a = f_ref[p, pl.ds(8 * r, 8), pl.ds(128 * h, 128)]
                b = f_ref[p + PAIRS, pl.ds(8 * r, 8), pl.ds(128 * h, 128)]
                both = (
                    jnp.where(low, a, pltpu.roll(b, 64, 1)),
                    jnp.where(low, pltpu.roll(a, 64, 1), b),
                )
                for o in range(2):
                    c = 2 * h + o
                    first, last = both[o][0:1], both[o][7:8]
                    out_ref[holder(r, c), pl.ds(8 * p, 8), :] = both[o]
                    if r == 0:
                        out_ref[holder(0, c), pl.ds(FIRST + p, 1), :] = first
                    if r == 3:
                        out_ref[holder(3, c), pl.ds(FIRST + p, 1), :] = last
                    if r < 3:
                        out_ref[holder(r + 1, c), pl.ds((FIRST if r < 2 else SECOND) + p, 1), :] = last
                    if r > 0:
                        out_ref[holder(r - 1, c), pl.ds(SECOND + p, 1), :] = first
                here = (lane % 64) // 2 == p
                ga = jnp.where(here, pltpu.roll(a, (2 * p - 63) % 128, 1), ga)
                gb = jnp.where(here, pltpu.roll(b, 2 * p + 1, 1), gb)
            near.append(jnp.where(low, ga, gb))
            far.append(pltpu.roll(jnp.where(low, gb, ga), 64, 1))
        zero = jnp.zeros((8, 128), jnp.float32)
        sides = (
            jnp.where(even, zero, near[0]),
            jnp.where(even, near[0], far[1]),
            jnp.where(even, far[0], near[1]),
            jnp.where(even, near[1], zero),
        )
        for c in range(4):
            moved = pltpu.roll(pltpu.roll(sides[c], 32, 1), 2, 0)
            kept = jnp.where(spare, moved, sides[c])
            out_ref[holder(r, c), pl.ds(SIDE, 6), :] = kept[0:6]


def edge_kernel(got_ref, edge_ref):
    groups = got_ref.shape[0]
    for group in range(groups):
        edge_ref[pl.ds(8 * group, 8), :] = got_ref[group, pl.ds(FIRST, 8), :]
        edge_ref[pl.ds(8 * groups + group, 1), :] = got_ref[group, pl.ds(FIRST + 8, 1), :]


def coef_kernel(place_ref, modes_ref, edge_ref, coef_ref):
    low = lanes_of() < 64
    block_row = row_group(place_ref[0])
    block_col = place_ref[0] // 4
    first = block_row == 0
    last = block_row == 3
    odd = block_col % 2 == 1
    right_half = block_col >= 2
    lane = lanes_of((8, 256))
    sub = subs_of((8, 256))
    for k in range(modes_ref.shape[0]):
        here = modes_ref[k, pl.ds(pl.multiple_of(8 * block_row, 8), 8), :]
        before = modes_ref[k, pl.ds(pl.multiple_of(8 * jnp.maximum(block_row - 1, 0), 8), 8), :]
        after = modes_ref[k, pl.ds(pl.multiple_of(8 * jnp.minimum(block_row + 1, 3), 8), 8), :]
        over = jnp.where(first, edge_ref[pl.ds(k, 1), :], before[7:8])
        under = jnp.where(last, edge_ref[pl.ds(k, 1), :], after[0:1])
        up = jnp.where(sub == 0, over, pltpu.roll(here, 1, 0))
        down = jnp.where(sub == 7, under, pltpu.roll(here, 7, 0))
        left = jnp.where(lane == 0, 0.0, pltpu.roll(here, 1, 1))
        right = jnp.where(lane == 255, 0.0, pltpu.roll(here, 255, 1))

        def both(x, y):
            x = 0.5 * (here + x)
            y = 0.5 * (here + y)
            x = jnp.where(right_half, x[:, 128:], x[:, :128])
            y = jnp.where(right_half, y[:, 128:], y[:, :128])
            return jnp.where(
                odd,
                jnp.where(low, pltpu.roll(x, 64, 1), y),
                jnp.where(low, x, pltpu.roll(y, 64, 1)),
            )

        coef_ref[k, pl.ds(0, 8), :] = both(up, down)
        coef_ref[k, pl.ds(8, 8), :] = both(left, right)


def load_kernel(place_ref, index_ref, got_ref, diff_ref):
    lane, sub = lanes_of(), subs_of()
    low = lane < 64
    block_row = row_group(place_ref[0])
    first = block_row == 0
    last = block_row == 3
    over_one = (sub == 0) & jnp.logical_not(first | last)
    over_two = (sub == 0) & last
    under = (sub == 7) & jnp.logical_not(last)
    inner_up = sub > 0
    inner_down = sub < 7

    def load(group, carry):
        tail = got_ref[group, pl.ds(ROWS - 8, 8), :]
        beside = jnp.where(
            sub < 6, pltpu.roll(tail, 6, 0), pltpu.roll(pltpu.roll(tail, 96, 1), 4, 0)
        )
        made = []
        for p in range(PAIRS):
            here = got_ref[group, pl.ds(8 * p, 8), :]
            one = got_ref[group, pl.ds(FIRST + p, 1), :]
            two = got_ref[group, pl.ds(SECOND + p, 1), :]
            above = jnp.where(over_one, one, jnp.where(over_two, two, 0.0))
            below = jnp.where(under, two, 0.0)
            up = here - jnp.where(inner_up, pltpu.roll(here, 1, 0), above)
            down = here - jnp.where(inner_down, pltpu.roll(here, 7, 0), below)
            left = here - jnp.where(
                lane % 64 == 0, pltpu.roll(beside, (128 - 2 * p) % 128, 1), pltpu.roll(here, 1, 1)
            )
            right = here - jnp.where(
                lane % 64 == 63, pltpu.roll(beside, 62 - 2 * p, 1), pltpu.roll(here, 127, 1)
            )
            vert = pltpu.roll(jnp.where(low, down, up), 64, 1)
            hori = pltpu.roll(jnp.where(low, right, left), 64, 1)
            made.append((p, jnp.where(low, up, vert), jnp.where(low, left, hori)))
            made.append((p + PAIRS, jnp.where(low, vert, down), jnp.where(low, hori, right)))
        for i, vert, hori in made:
            term = index_ref[group * (2 * PAIRS) + i]
            diff_ref[term, pl.ds(0, 8), :] = vert
            diff_ref[term, pl.ds(8, 8), :] = hori
        return carry

    lax.fori_loop(0, got_ref.shape[0], load, 0, unroll=4)


def mix_kernel(
    place_ref, index_ref, own_ref, weight_ref, diff_ref, edge_ref, coef_ref, out_ref, diff, total
):
    lane, sub = lanes_of(), subs_of()
    low = lane < 64
    groups = out_ref.shape[0]
    slots = groups * 2 * PAIRS
    first = row_group(place_ref[0]) == 0
    last = row_group(place_ref[0]) == 3
    meets = jnp.where((low & (sub == 0) & first) | ((lane >= 64) & (sub == 7) & last), 1.0, 0.0)

    def own(group, carry):
        edge = edge_ref[pl.ds(pl.multiple_of(8 * group, 8), 8), :]
        more = edge_ref[pl.ds(8 * groups + group, 1), :]
        rows = [edge[p : p + 1] for p in range(8)] + [more]
        coef_v = coef_ref[0, pl.ds(0, 8), :]
        coef_h = coef_ref[0, pl.ds(8, 8), :]
        made = []
        for p in range(PAIRS):
            beyond = jnp.broadcast_to(rows[p], (8, 128))
            turned = pltpu.roll(beyond, 64, 1)
            for o in range(2):
                term = index_ref[group * (2 * PAIRS) + o * PAIRS + p]
                mine = jnp.where(first, beyond, turned) if o == 0 else jnp.where(first, turned, beyond)
                vert = diff_ref[term, pl.ds(0, 8), :] - meets * mine
                hori = diff_ref[term, pl.ds(8, 8), :]
                made.append((term, vert, hori, own_ref[term] * (coef_v * vert + coef_h * hori)))
        for term, vert, hori, value in made:
            diff[term, pl.ds(0, 8), :] = vert
            diff[term, pl.ds(8, 8), :] = hori
            total[term] = value
        return carry

    lax.fori_loop(0, groups, own, 0, unroll=4)

    def couple(step, carry):
        terms = [6 * step + i for i in range(6)]
        uppers, gains, mine = [], [], []
        for term in terms:
            vert = diff[term, pl.ds(0, 8), :]
            hori = diff[term, pl.ds(8, 8), :]
            parts = []
            for v in range(VARS):
                coef_v = coef_ref[v + 1, pl.ds(0, 8), :]
                coef_h = coef_ref[v + 1, pl.ds(8, 8), :]
                upper = index_ref[slots + term * VARS + v]
                uppers.append(upper)
                parts.append(
                    weight_ref[term, pl.ds(v, 1), :]
                    * (coef_v * diff[upper, pl.ds(0, 8), :] + coef_h * diff[upper, pl.ds(8, 8), :])
                )
                gains.append(weight_ref[term, pl.ds(VARS + v, 1), :] * (coef_v * vert + coef_h * hori))
            while len(parts) > 1:
                parts = [x + y for x, y in zip(parts[::2], parts[1::2])] + parts[len(parts) // 2 * 2 :]
            mine.append(parts[0])
        for i, term in enumerate(terms):
            total[term] = total[term] + mine[i]
            sums = [total[uppers[i * VARS + v]] + gains[i * VARS + v] for v in range(VARS)]
            for v in range(VARS):
                total[uppers[i * VARS + v]] = sums[v]
        return carry

    lax.fori_loop(0, LOWER // 6, couple, 0)

    def store(group, carry):
        made = []
        for p in range(PAIRS):
            a = total[index_ref[group * (2 * PAIRS) + p]]
            b = total[index_ref[group * (2 * PAIRS) + PAIRS + p]]
            made.append(jnp.where(low, a, b) + pltpu.roll(jnp.where(low, b, a), 64, 1))
        for p in range(PAIRS):
            out_ref[group, pl.ds(8 * p, 8), :] = made[p]
        return carry

    lax.fori_loop(0, groups, store, 0, unroll=8)


def unpack_kernel(got_ref, out_ref):
    low = lanes_of() < 64
    for r in range(4):
        for h in range(2):
            for p in range(PAIRS):
                one = got_ref[holder(r, 2 * h), pl.ds(8 * p, 8), :]
                two = got_ref[holder(r, 2 * h + 1), pl.ds(8 * p, 8), :]
                out_ref[p, pl.ds(8 * r, 8), pl.ds(128 * h, 128)] = jnp.where(
                    low, one, pltpu.roll(two, 64, 1)
                )
                out_ref[p + PAIRS, pl.ds(8 * r, 8), pl.ds(128 * h, 128)] = jnp.where(
                    low, pltpu.roll(one, 64, 1), two
                )


def vmem():
    return pl.BlockSpec(memory_space=pltpu.VMEM)


def smem():
    return pl.BlockSpec(memory_space=pltpu.SMEM)


def f32(*shape):
    return jax.ShapeDtypeStruct(shape, jnp.float32)


PARAMS = pltpu.CompilerParams(vmem_limit_bytes=32 * 1024 * 1024)


def cost(micros):
    return pl.CostEstimate(flops=0, bytes_accessed=micros * 3000000, transcendentals=0)


def pack(fields, groups):
    return pl.pallas_call(
        pack_kernel,
        out_shape=f32(groups, ROWS, 128),
        in_specs=[vmem()],
        out_specs=vmem(),
        compiler_params=PARAMS,
        cost_estimate=cost(2),
    )(fields)


def edges(got):
    return pl.pallas_call(
        edge_kernel,
        out_shape=f32(got.shape[0] * PAIRS, 128),
        in_specs=[vmem()],
        out_specs=vmem(),
        compiler_params=PARAMS,
        cost_estimate=cost(1),
    )(got)


def coefs(place, modes, edge):
    return pl.pallas_call(
        coef_kernel,
        out_shape=f32(modes.shape[0], 16, 128),
        in_specs=[smem(), vmem(), vmem()],
        out_specs=vmem(),
        compiler_params=PARAMS,
        cost_estimate=cost(1),
    )(place, modes, edge)


def load(place, index, got):
    groups = got.shape[0]
    return pl.pallas_call(
        load_kernel,
        out_shape=f32(groups * 2 * PAIRS, 16, 128),
        in_specs=[smem(), smem(), vmem()],
        out_specs=vmem(),
        compiler_params=PARAMS,
        cost_estimate=cost(4),
    )(place, index, got)


def mix(place, index, own, weights, diff, edge, coef):
    slots = diff.shape[0]
    groups = slots // (2 * PAIRS)
    return pl.pallas_call(
        mix_kernel,
        out_shape=f32(groups, BLOCK, 128),
        in_specs=[smem(), smem(), smem()] + [vmem()] * 4,
        out_specs=vmem(),
        scratch_shapes=[
            pltpu.VMEM((slots, 16, 128), jnp.float32),
            pltpu.VMEM((slots, 8, 128), jnp.float32),
        ],
        compiler_params=PARAMS,
        cost_estimate=cost(5),
    )(place, index, own, weights, diff, edge, coef)


def unpack(got, shape):
    return pl.pallas_call(
        unpack_kernel,
        out_shape=f32(*shape),
        in_specs=[vmem()],
        out_specs=vmem(),
        compiler_params=PARAMS,
        cost_estimate=cost(1),
    )(got)


def tables(pair_list, pair_value, assign):
    terms = assign.shape[0]
    row, col, mode = pair_list[:, 0:1], pair_list[:, 1:2], pair_list[:, 2:3]
    at = jnp.minimum(row, col) == jnp.arange(terms, dtype=jnp.int32)[None, :]
    kinds = jnp.arange(1 + 3 * VARS, dtype=jnp.int32)[None, :]
    wanted = jnp.where(kinds <= VARS, kinds, (kinds - 1) % VARS + 1)
    side = jnp.where(kinds <= VARS, row <= col, jnp.where(kinds <= 2 * VARS, row > col, row < col))
    value = jnp.where(kinds <= 2 * VARS, pair_value[:, None], col.astype(jnp.float32))
    value = jnp.where((mode == wanted) & side, value, 0.0)
    found = lax.dot_general(
        at.astype(jnp.float32),
        value,
        (((0,), (0,)), ((), ())),
        precision=lax.Precision.HIGHEST,
        preferred_element_type=jnp.float32,
    )
    coupled = jnp.pad(found[:LOWER, 1 : 1 + 2 * VARS], ((0, 0), (0, 4)))
    uppers = jnp.round(found[:LOWER, 1 + 2 * VARS :]).astype(jnp.int32).reshape(-1)
    weights = jnp.broadcast_to(coupled[:, :, None], coupled.shape + (128,))
    return jnp.concatenate([assign, uppers]), found[:, 0], weights


def shards(fields, modes, pair_list, pair_value, assign):
    groups = lax.axis_size("term")
    count = lax.axis_size("space")
    passes = []
    for c in range(groups // 4):
        for s in range(count - 1):
            lower, upper = holder(0, c) * count + s + 1, holder(3, c) * count + s
            passes += [(lower, upper), (upper, lower)]
    place = lax.axis_index("term").astype(jnp.int32).reshape(1)
    sent = pack(fields, groups)
    sent, modes = lax.optimization_barrier((sent, modes))
    got = lax.all_to_all(sent, "term", 0, 0, tiled=True)
    index, own, weights = tables(pair_list, pair_value, assign)
    edge = jnp.where(row_group(place[0]) == 0, modes[:, 0], modes[:, modes.shape[1] - 1])
    coef = coefs(place, modes, lax.ppermute(edge, ("term", "space"), passes))
    beyond = lax.ppermute(edges(got), ("term", "space"), passes)
    diff = load(place, index, got)
    mixed = mix(place, index, own, weights, diff, beyond, coef)
    back = lax.all_to_all(mixed, "term", 0, 0, tiled=True)
    return unpack(back, fields.shape)


def solution(mesh):
    return jax.shard_map(
        shards,
        mesh=mesh,
        in_specs=(P("term", "space", None), P(None, "space", None), P(), P(), P()),
        out_specs=P("term", "space", None),
        check_vma=False,
    )
```

```python
import jax
import jax.numpy as jnp
from jax import lax
from jax.experimental import pallas as pl
from jax.experimental.pallas import tpu as pltpu
from jax.sharding import PartitionSpec as P

PAIRS = 9
BLOCK = 8 * PAIRS
ROWS = 96
FIRST = 72
SECOND = 81
SIDE = 90
LOWER = 66
VARS = 10


def holder(r, c):
    return 4 * c + (r ^ c)


def mask_at(space):
    return (space >> 1 & 1) * 8 + (space & 1) * 3


def here():
    mask = mask_at(lax.axis_index("space"))
    return mask, lax.axis_index("term") ^ mask


def row_group(place):
    return (place & 3) ^ (place >> 2)


def lanes_of(shape=(8, 128)):
    return lax.broadcasted_iota(jnp.int32, shape, 1)


def subs_of(shape=(8, 128)):
    return lax.broadcasted_iota(jnp.int32, shape, 0)


def pack_kernel(f_ref, out_ref):
    lane = lanes_of()
    low = lane < 64
    even = lane % 2 == 0
    spare = lane % 64 >= 32
    mask, _ = here()
    for r in range(4):
        near, far = [], []
        for h in range(2):
            ga = jnp.zeros((8, 128), jnp.float32)
            gb = jnp.zeros((8, 128), jnp.float32)
            for p in range(PAIRS):
                a = f_ref[p, pl.ds(8 * r, 8), pl.ds(128 * h, 128)]
                b = f_ref[p + PAIRS, pl.ds(8 * r, 8), pl.ds(128 * h, 128)]
                both = (
                    jnp.where(low, a, pltpu.roll(b, 64, 1)),
                    jnp.where(low, pltpu.roll(a, 64, 1), b),
                )
                for o in range(2):
                    c = 2 * h + o
                    first, last = both[o][0:1], both[o][7:8]
                    out_ref[holder(r, c) ^ mask, pl.ds(8 * p, 8), :] = both[o]
                    if r == 0:
                        out_ref[holder(0, c) ^ mask, pl.ds(FIRST + p, 1), :] = first
                    if r == 3:
                        out_ref[holder(3, c) ^ mask, pl.ds(FIRST + p, 1), :] = last
                    if r < 3:
                        out_ref[holder(r + 1, c) ^ mask, pl.ds((FIRST if r < 2 else SECOND) + p, 1), :] = last
                    if r > 0:
                        out_ref[holder(r - 1, c) ^ mask, pl.ds(SECOND + p, 1), :] = first
                pair = (lane % 64) // 2 == p
                ga = jnp.where(pair, pltpu.roll(a, (2 * p - 63) % 128, 1), ga)
                gb = jnp.where(pair, pltpu.roll(b, 2 * p + 1, 1), gb)
            near.append(jnp.where(low, ga, gb))
            far.append(pltpu.roll(jnp.where(low, gb, ga), 64, 1))
        zero = jnp.zeros((8, 128), jnp.float32)
        sides = (
            jnp.where(even, zero, near[0]),
            jnp.where(even, near[0], far[1]),
            jnp.where(even, far[0], near[1]),
            jnp.where(even, near[1], zero),
        )
        for c in range(4):
            moved = pltpu.roll(pltpu.roll(sides[c], 32, 1), 2, 0)
            kept = jnp.where(spare, moved, sides[c])
            out_ref[holder(r, c) ^ mask, pl.ds(SIDE, 6), :] = kept[0:6]


def edge_kernel(got_ref, edge_ref):
    groups = got_ref.shape[0]
    for group in range(groups):
        edge_ref[pl.ds(8 * group, 8), :] = got_ref[group, pl.ds(FIRST, 8), :]
        edge_ref[pl.ds(8 * groups + group, 1), :] = got_ref[group, pl.ds(FIRST + 8, 1), :]


def coef_kernel(modes_ref, edge_ref, weight_ref, coef_ref):
    _, place = here()
    low = lanes_of() < 64
    block_row = row_group(place)
    block_col = place >> 2
    first = block_row == 0
    last = block_row == 3
    odd = block_col % 2 == 1
    right_half = block_col >= 2
    lane = lanes_of((8, 256))
    sub = subs_of((8, 256))
    for k in range(modes_ref.shape[0]):
        cells = modes_ref[k, pl.ds(pl.multiple_of(8 * block_row, 8), 8), :]
        before = modes_ref[k, pl.ds(pl.multiple_of(8 * jnp.maximum(block_row - 1, 0), 8), 8), :]
        after = modes_ref[k, pl.ds(pl.multiple_of(8 * jnp.minimum(block_row + 1, 3), 8), 8), :]
        over = jnp.where(first, edge_ref[pl.ds(k, 1), :], before[7:8])
        under = jnp.where(last, edge_ref[pl.ds(k, 1), :], after[0:1])
        up = jnp.where(sub == 0, over, pltpu.roll(cells, 1, 0))
        down = jnp.where(sub == 7, under, pltpu.roll(cells, 7, 0))
        left = jnp.where(lane == 0, 0.0, pltpu.roll(cells, 1, 1))
        right = jnp.where(lane == 255, 0.0, pltpu.roll(cells, 255, 1))

        def both(x, y):
            x = 0.5 * (cells + x)
            y = 0.5 * (cells + y)
            x = jnp.where(right_half, x[:, 128:], x[:, :128])
            y = jnp.where(right_half, y[:, 128:], y[:, :128])
            return jnp.where(
                odd,
                jnp.where(low, pltpu.roll(x, 64, 1), y),
                jnp.where(low, x, pltpu.roll(y, 64, 1)),
            )

        coef_ref[k, pl.ds(0, 8), :] = both(up, down)
        coef_ref[k, pl.ds(8, 8), :] = both(left, right)


def load_kernel(index_ref, got_ref, diff_ref):
    _, place = here()
    lane, sub = lanes_of(), subs_of()
    low = lane < 64
    block_row = row_group(place)
    first = block_row == 0
    last = block_row == 3
    over_one = (sub == 0) & jnp.logical_not(first | last)
    over_two = (sub == 0) & last
    under = (sub == 7) & jnp.logical_not(last)
    inner_up = sub > 0
    inner_down = sub < 7

    def load(group, carry):
        tail = got_ref[group, pl.ds(ROWS - 8, 8), :]
        beside = jnp.where(
            sub < 6, pltpu.roll(tail, 6, 0), pltpu.roll(pltpu.roll(tail, 96, 1), 4, 0)
        )
        made = []
        for p in range(PAIRS):
            cells = got_ref[group, pl.ds(8 * p, 8), :]
            one = got_ref[group, pl.ds(FIRST + p, 1), :]
            two = got_ref[group, pl.ds(SECOND + p, 1), :]
            above = jnp.where(over_one, one, jnp.where(over_two, two, 0.0))
            below = jnp.where(under, two, 0.0)
            up = cells - jnp.where(inner_up, pltpu.roll(cells, 1, 0), above)
            down = cells - jnp.where(inner_down, pltpu.roll(cells, 7, 0), below)
            left = cells - jnp.where(
                lane % 64 == 0, pltpu.roll(beside, (128 - 2 * p) % 128, 1), pltpu.roll(cells, 1, 1)
            )
            right = cells - jnp.where(
                lane % 64 == 63, pltpu.roll(beside, 62 - 2 * p, 1), pltpu.roll(cells, 127, 1)
            )
            vert = pltpu.roll(jnp.where(low, down, up), 64, 1)
            hori = pltpu.roll(jnp.where(low, right, left), 64, 1)
            made.append((p, jnp.where(low, up, vert), jnp.where(low, left, hori)))
            made.append((p + PAIRS, jnp.where(low, vert, down), jnp.where(low, hori, right)))
        for i, vert, hori in made:
            term = index_ref[group * (2 * PAIRS) + i]
            diff_ref[term, pl.ds(0, 8), :] = vert
            diff_ref[term, pl.ds(8, 8), :] = hori
        return carry

    lax.fori_loop(0, got_ref.shape[0], load, 0, unroll=4)


def mix_kernel(
    index_ref, own_ref, weight_ref, diff_ref, edge_ref, coef_ref, out_ref, diff, total
):
    _, place = here()
    lane, sub = lanes_of(), subs_of()
    low = lane < 64
    groups = out_ref.shape[0]
    slots = groups * 2 * PAIRS
    first = row_group(place) == 0
    last = row_group(place) == 3
    meets = jnp.where((low & (sub == 0) & first) | ((lane >= 64) & (sub == 7) & last), 1.0, 0.0)

    def own(group, carry):
        edge = edge_ref[pl.ds(pl.multiple_of(8 * group, 8), 8), :]
        more = edge_ref[pl.ds(8 * groups + group, 1), :]
        rows = [edge[p : p + 1] for p in range(8)] + [more]
        coef_v = coef_ref[0, pl.ds(0, 8), :]
        coef_h = coef_ref[0, pl.ds(8, 8), :]
        made = []
        for p in range(PAIRS):
            beyond = jnp.broadcast_to(rows[p], (8, 128))
            turned = pltpu.roll(beyond, 64, 1)
            for o in range(2):
                term = index_ref[group * (2 * PAIRS) + o * PAIRS + p]
                mine = jnp.where(first, beyond, turned) if o == 0 else jnp.where(first, turned, beyond)
                vert = diff_ref[term, pl.ds(0, 8), :] - meets * mine
                hori = diff_ref[term, pl.ds(8, 8), :]
                made.append((term, vert, hori, own_ref[term] * (coef_v * vert + coef_h * hori)))
        for term, vert, hori, value in made:
            diff[term, pl.ds(0, 8), :] = vert
            diff[term, pl.ds(8, 8), :] = hori
            total[term] = value
        return carry

    lax.fori_loop(0, groups, own, 0, unroll=4)

    def couple(step, carry):
        terms = [6 * step + i for i in range(6)]
        uppers, gains, mine = [], [], []
        for term in terms:
            vert = diff[term, pl.ds(0, 8), :]
            hori = diff[term, pl.ds(8, 8), :]
            parts = []
            for v in range(VARS):
                coef_v = coef_ref[v + 1, pl.ds(0, 8), :]
                coef_h = coef_ref[v + 1, pl.ds(8, 8), :]
                upper = index_ref[slots + term * VARS + v]
                uppers.append(upper)
                parts.append(
                    weight_ref[term, pl.ds(v, 1), :]
                    * (coef_v * diff[upper, pl.ds(0, 8), :] + coef_h * diff[upper, pl.ds(8, 8), :])
                )
                gains.append(weight_ref[term, pl.ds(VARS + v, 1), :] * (coef_v * vert + coef_h * hori))
            while len(parts) > 1:
                parts = [x + y for x, y in zip(parts[::2], parts[1::2])] + parts[len(parts) // 2 * 2 :]
            mine.append(parts[0])
        for i, term in enumerate(terms):
            total[term] = total[term] + mine[i]
            sums = [total[uppers[i * VARS + v]] + gains[i * VARS + v] for v in range(VARS)]
            for v in range(VARS):
                total[uppers[i * VARS + v]] = sums[v]
        return carry

    lax.fori_loop(0, LOWER // 6, couple, 0)

    def store(group, carry):
        made = []
        for p in range(PAIRS):
            a = total[index_ref[group * (2 * PAIRS) + p]]
            b = total[index_ref[group * (2 * PAIRS) + PAIRS + p]]
            made.append(jnp.where(low, a, b) + pltpu.roll(jnp.where(low, b, a), 64, 1))
        for p in range(PAIRS):
            out_ref[group, pl.ds(8 * p, 8), :] = made[p]
        return carry

    lax.fori_loop(0, groups, store, 0, unroll=8)


def unpack_kernel(got_ref, out_ref):
    low = lanes_of() < 64
    mask, _ = here()
    for r in range(4):
        for h in range(2):
            for p in range(PAIRS):
                one = got_ref[holder(r, 2 * h) ^ mask, pl.ds(8 * p, 8), :]
                two = got_ref[holder(r, 2 * h + 1) ^ mask, pl.ds(8 * p, 8), :]
                out_ref[p, pl.ds(8 * r, 8), pl.ds(128 * h, 128)] = jnp.where(
                    low, one, pltpu.roll(two, 64, 1)
                )
                out_ref[p + PAIRS, pl.ds(8 * r, 8), pl.ds(128 * h, 128)] = jnp.where(
                    low, pltpu.roll(one, 64, 1), two
                )


def vmem():
    return pl.BlockSpec(memory_space=pltpu.VMEM)


def smem():
    return pl.BlockSpec(memory_space=pltpu.SMEM)


def f32(*shape):
    return jax.ShapeDtypeStruct(shape, jnp.float32)


PARAMS = pltpu.CompilerParams(vmem_limit_bytes=32 * 1024 * 1024)


def cost(micros):
    return pl.CostEstimate(flops=0, bytes_accessed=micros * 3000000, transcendentals=0)


def pack(fields, groups):
    return pl.pallas_call(
        pack_kernel,
        out_shape=f32(groups, ROWS, 128),
        in_specs=[vmem()],
        out_specs=vmem(),
        compiler_params=PARAMS,
        cost_estimate=cost(2),
    )(fields)


def edges(got):
    return pl.pallas_call(
        edge_kernel,
        out_shape=f32(got.shape[0] * PAIRS, 128),
        in_specs=[vmem()],
        out_specs=vmem(),
        compiler_params=PARAMS,
        cost_estimate=cost(1),
    )(got)


def coefs(modes, edge, weights):
    return pl.pallas_call(
        coef_kernel,
        out_shape=f32(modes.shape[0], 16, 128),
        in_specs=[vmem(), vmem(), pl.BlockSpec(memory_space=pl.ANY)],
        out_specs=vmem(),
        compiler_params=PARAMS,
        cost_estimate=cost(1),
    )(modes, edge, weights)


def load(index, got):
    groups = got.shape[0]
    return pl.pallas_call(
        load_kernel,
        out_shape=f32(groups * 2 * PAIRS, 16, 128),
        in_specs=[smem(), vmem()],
        out_specs=vmem(),
        compiler_params=PARAMS,
        cost_estimate=cost(4),
    )(index, got)


def mix(index, own, weights, diff, edge, coef):
    slots = diff.shape[0]
    groups = slots // (2 * PAIRS)
    return pl.pallas_call(
        mix_kernel,
        out_shape=f32(groups, BLOCK, 128),
        in_specs=[smem(), smem()] + [vmem()] * 4,
        out_specs=vmem(),
        scratch_shapes=[
            pltpu.VMEM((slots, 16, 128), jnp.float32),
            pltpu.VMEM((slots, 8, 128), jnp.float32),
        ],
        compiler_params=PARAMS,
        cost_estimate=cost(5),
    )(index, own, weights, diff, edge, coef)


def unpack(got, shape):
    return pl.pallas_call(
        unpack_kernel,
        out_shape=f32(*shape),
        in_specs=[vmem()],
        out_specs=vmem(),
        compiler_params=PARAMS,
        cost_estimate=cost(1),
    )(got)


def tables(pair_list, pair_value, assign):
    terms = assign.shape[0]
    row, col, mode = pair_list[:, 0:1], pair_list[:, 1:2], pair_list[:, 2:3]
    at = jnp.minimum(row, col) == jnp.arange(terms, dtype=jnp.int32)[None, :]
    kinds = jnp.arange(1 + 3 * VARS, dtype=jnp.int32)[None, :]
    wanted = jnp.where(kinds <= VARS, kinds, (kinds - 1) % VARS + 1)
    side = jnp.where(kinds <= VARS, row <= col, jnp.where(kinds <= 2 * VARS, row > col, row < col))
    value = jnp.where(kinds <= 2 * VARS, pair_value[:, None], col.astype(jnp.float32))
    value = jnp.where((mode == wanted) & side, value, 0.0)
    found = lax.dot_general(
        at.astype(jnp.float32),
        value,
        (((0,), (0,)), ((), ())),
        precision=lax.Precision.HIGHEST,
        preferred_element_type=jnp.float32,
    )
    coupled = jnp.pad(found[:LOWER, 1 : 1 + 2 * VARS], ((0, 0), (0, 4)))
    uppers = jnp.round(found[:LOWER, 1 + 2 * VARS :]).astype(jnp.int32).reshape(-1)
    weights = jnp.broadcast_to(coupled[:, :, None], coupled.shape + (128,))
    return jnp.concatenate([assign, uppers]), found[:, 0], weights


def shards(fields, modes, pair_list, pair_value, assign):
    groups = lax.axis_size("term")
    count = lax.axis_size("space")
    passes = []
    for c in range(groups // 4):
        for s in range(count - 1):
            lower = (holder(0, c) ^ mask_at(s + 1)) * count + s + 1
            upper = (holder(3, c) ^ mask_at(s)) * count + s
            passes += [(lower, upper), (upper, lower)]
    sent = pack(fields, groups)
    sent, modes = lax.optimization_barrier((sent, modes))
    got = lax.all_to_all(sent, "term", 0, 0, tiled=True)
    index, own, weights = tables(pair_list, pair_value, assign)
    _, place = here()
    edge = jnp.where(row_group(place) == 0, modes[:, 0], modes[:, modes.shape[1] - 1])
    coef = coefs(modes, lax.ppermute(edge, ("term", "space"), passes), weights)
    got, coef, index = lax.optimization_barrier((got, coef, index))
    beyond = lax.ppermute(edges(got), ("term", "space"), passes)
    diff = load(index, got)
    mixed = mix(index, own, weights, diff, beyond, coef)
    back = lax.all_to_all(mixed, "term", 0, 0, tiled=True)
    return unpack(back, fields.shape)


def solution(mesh):
    return jax.shard_map(
        shards,
        mesh=mesh,
        in_specs=(P("term", "space", None), P(None, "space", None), P(), P(), P()),
        out_specs=P("term", "space", None),
        check_vma=False,
    )
```

```python
import jax
import jax.numpy as jnp
from jax import lax
from jax.experimental import pallas as pl
from jax.experimental.pallas import tpu as pltpu
from jax.sharding import PartitionSpec as P

PAIRS = 9
BLOCK = 8 * PAIRS
ROWS = 96
FIRST = 72
SECOND = 81
SIDE = 90
LOWER = 66
VARS = 10


def holder(r, c):
    return 4 * c + (r ^ c)


def mask_at(space):
    return (space >> 1 & 1) * 8 + (space & 1) * 3


def here():
    mask = mask_at(lax.axis_index("space"))
    return mask, lax.axis_index("term") ^ mask


def row_group(place):
    return (place & 3) ^ (place >> 2)


def lanes_of(shape=(8, 128)):
    return lax.broadcasted_iota(jnp.int32, shape, 1)


def subs_of(shape=(8, 128)):
    return lax.broadcasted_iota(jnp.int32, shape, 0)


def pack_kernel(f_ref, sent_ref, out_ref, out_sem):
    lane = lanes_of()
    low = lane < 64
    even = lane % 2 == 0
    spare = lane % 64 >= 32
    mask, _ = here()

    def send(r, c):
        to = holder(r, c) ^ mask
        return pltpu.make_async_copy(out_ref.at[to], sent_ref.at[to], out_sem.at[4 * r + c])

    for r in range(4):
        near, far = [], []
        for h in range(2):
            ga = jnp.zeros((8, 128), jnp.float32)
            gb = jnp.zeros((8, 128), jnp.float32)
            for p in range(PAIRS):
                a = f_ref[p, pl.ds(8 * r, 8), pl.ds(128 * h, 128)]
                b = f_ref[p + PAIRS, pl.ds(8 * r, 8), pl.ds(128 * h, 128)]
                both = (
                    jnp.where(low, a, pltpu.roll(b, 64, 1)),
                    jnp.where(low, pltpu.roll(a, 64, 1), b),
                )
                for o in range(2):
                    c = 2 * h + o
                    first, last = both[o][0:1], both[o][7:8]
                    out_ref[holder(r, c) ^ mask, pl.ds(8 * p, 8), :] = both[o]
                    if r == 0:
                        out_ref[holder(0, c) ^ mask, pl.ds(FIRST + p, 1), :] = first
                    if r == 3:
                        out_ref[holder(3, c) ^ mask, pl.ds(FIRST + p, 1), :] = last
                    if r < 3:
                        out_ref[holder(r + 1, c) ^ mask, pl.ds((FIRST if r < 2 else SECOND) + p, 1), :] = last
                    if r > 0:
                        out_ref[holder(r - 1, c) ^ mask, pl.ds(SECOND + p, 1), :] = first
                pair = (lane % 64) // 2 == p
                ga = jnp.where(pair, pltpu.roll(a, (2 * p - 63) % 128, 1), ga)
                gb = jnp.where(pair, pltpu.roll(b, 2 * p + 1, 1), gb)
            near.append(jnp.where(low, ga, gb))
            far.append(pltpu.roll(jnp.where(low, gb, ga), 64, 1))
        zero = jnp.zeros((8, 128), jnp.float32)
        sides = (
            jnp.where(even, zero, near[0]),
            jnp.where(even, near[0], far[1]),
            jnp.where(even, far[0], near[1]),
            jnp.where(even, near[1], zero),
        )
        for c in range(4):
            moved = pltpu.roll(pltpu.roll(sides[c], 32, 1), 2, 0)
            kept = jnp.where(spare, moved, sides[c])
            out_ref[holder(r, c) ^ mask, pl.ds(SIDE, 6), :] = kept[0:6]
        for done in ((r - 1, r) if r == 3 else (r - 1,)):
            if done >= 0:
                for c in range(4):
                    send(done, c).start()
    for r in range(4):
        for c in range(4):
            send(r, c).wait()


def edge_kernel(got_ref, edge_ref):
    groups = got_ref.shape[0]
    for group in range(groups):
        edge_ref[pl.ds(8 * group, 8), :] = got_ref[group, pl.ds(FIRST, 8), :]
        edge_ref[pl.ds(8 * groups + group, 1), :] = got_ref[group, pl.ds(FIRST + 8, 1), :]


def coef_kernel(modes_ref, edge_ref, weight_ref, coef_ref):
    _, place = here()
    low = lanes_of() < 64
    block_row = row_group(place)
    block_col = place >> 2
    first = block_row == 0
    last = block_row == 3
    odd = block_col % 2 == 1
    right_half = block_col >= 2
    lane = lanes_of((8, 256))
    sub = subs_of((8, 256))
    for k in range(modes_ref.shape[0]):
        cells = modes_ref[k, pl.ds(pl.multiple_of(8 * block_row, 8), 8), :]
        before = modes_ref[k, pl.ds(pl.multiple_of(8 * jnp.maximum(block_row - 1, 0), 8), 8), :]
        after = modes_ref[k, pl.ds(pl.multiple_of(8 * jnp.minimum(block_row + 1, 3), 8), 8), :]
        over = jnp.where(first, edge_ref[pl.ds(k, 1), :], before[7:8])
        under = jnp.where(last, edge_ref[pl.ds(k, 1), :], after[0:1])
        up = jnp.where(sub == 0, over, pltpu.roll(cells, 1, 0))
        down = jnp.where(sub == 7, under, pltpu.roll(cells, 7, 0))
        left = jnp.where(lane == 0, 0.0, pltpu.roll(cells, 1, 1))
        right = jnp.where(lane == 255, 0.0, pltpu.roll(cells, 255, 1))

        def both(x, y):
            x = 0.5 * (cells + x)
            y = 0.5 * (cells + y)
            x = jnp.where(right_half, x[:, 128:], x[:, :128])
            y = jnp.where(right_half, y[:, 128:], y[:, :128])
            return jnp.where(
                odd,
                jnp.where(low, pltpu.roll(x, 64, 1), y),
                jnp.where(low, x, pltpu.roll(y, 64, 1)),
            )

        coef_ref[k, pl.ds(0, 8), :] = both(up, down)
        coef_ref[k, pl.ds(8, 8), :] = both(left, right)


def load_kernel(own_ref, got_ref, coef_ref, diff_ref, total_ref):
    _, place = here()
    lane, sub = lanes_of(), subs_of()
    low = lane < 64
    block_row = row_group(place)
    first = block_row == 0
    last = block_row == 3
    over_one = (sub == 0) & jnp.logical_not(first | last)
    over_two = (sub == 0) & last
    under = (sub == 7) & jnp.logical_not(last)
    inner_up = sub > 0
    inner_down = sub < 7

    def load(group, carry):
        tail = got_ref[group, pl.ds(ROWS - 8, 8), :]
        beside = jnp.where(
            sub < 6, pltpu.roll(tail, 6, 0), pltpu.roll(pltpu.roll(tail, 96, 1), 4, 0)
        )
        made = []
        for p in range(PAIRS):
            cells = got_ref[group, pl.ds(8 * p, 8), :]
            one = got_ref[group, pl.ds(FIRST + p, 1), :]
            two = got_ref[group, pl.ds(SECOND + p, 1), :]
            above = jnp.where(over_one, one, jnp.where(over_two, two, 0.0))
            below = jnp.where(under, two, 0.0)
            up = cells - jnp.where(inner_up, pltpu.roll(cells, 1, 0), above)
            down = cells - jnp.where(inner_down, pltpu.roll(cells, 7, 0), below)
            left = cells - jnp.where(
                lane % 64 == 0, pltpu.roll(beside, (128 - 2 * p) % 128, 1), pltpu.roll(cells, 1, 1)
            )
            right = cells - jnp.where(
                lane % 64 == 63, pltpu.roll(beside, 62 - 2 * p, 1), pltpu.roll(cells, 127, 1)
            )
            vert = pltpu.roll(jnp.where(low, down, up), 64, 1)
            hori = pltpu.roll(jnp.where(low, right, left), 64, 1)
            made.append((p, jnp.where(low, up, vert), jnp.where(low, left, hori)))
            made.append((p + PAIRS, jnp.where(low, vert, down), jnp.where(low, hori, right)))
        coef_v = coef_ref[0, pl.ds(0, 8), :]
        coef_h = coef_ref[0, pl.ds(8, 8), :]
        for i, vert, hori in made:
            slot = group * (2 * PAIRS) + i
            diff_ref[slot, pl.ds(0, 8), :] = vert
            diff_ref[slot, pl.ds(8, 8), :] = hori
            total_ref[slot] = own_ref[pl.ds(slot, 1), :] * (coef_v * vert + coef_h * hori)
        return carry

    lax.fori_loop(0, got_ref.shape[0], load, 0, unroll=2)


def mix_kernel(
    place_ref, own_ref, weight_ref, diff_ref, start_ref, edge_ref, coef_ref, out_ref, diff, total, places, sem
):
    copy = pltpu.make_async_copy(place_ref, places, sem)
    copy.start()
    _, place = here()
    lane, sub = lanes_of(), subs_of()
    low = lane < 64
    groups = out_ref.shape[0]
    first = row_group(place) == 0
    last = row_group(place) == 3
    meets = jnp.where((low & (sub == 0) & first) | ((lane >= 64) & (sub == 7) & last), 1.0, 0.0)

    def patch(group, carry):
        edge = edge_ref[pl.ds(pl.multiple_of(8 * group, 8), 8), :]
        more = edge_ref[pl.ds(8 * groups + group, 1), :]
        rows = []
        for part in (edge, more):
            turned = pltpu.roll(part, 64, 1)
            rows.append((jnp.where(first, part, turned), jnp.where(first, turned, part)))
        coef_v = coef_ref[0, pl.ds(0, 8), :]
        made = []
        for p in range(PAIRS):
            for o in range(2):
                slot = group * (2 * PAIRS) + o * PAIRS + p
                beyond = meets * (rows[0][o][p : p + 1] if p < 8 else rows[1][o])
                vert = diff_ref[slot, pl.ds(0, 8), :] - beyond
                hori = diff_ref[slot, pl.ds(8, 8), :]
                made.append((slot, vert, hori, start_ref[slot] - own_ref[pl.ds(slot, 1), :] * (coef_v * beyond)))
        for slot, vert, hori, value in made:
            diff[slot, pl.ds(0, 8), :] = vert
            diff[slot, pl.ds(8, 8), :] = hori
            total[slot] = value
        return carry

    lax.fori_loop(0, groups, patch, 0, unroll=4)
    copy.wait()

    def couple(step, carry):
        terms = [6 * step + i for i in range(6)]
        uppers, gains, mine = [], [], []
        for term in terms:
            lower = places[term]
            vert = diff[lower, pl.ds(0, 8), :]
            hori = diff[lower, pl.ds(8, 8), :]
            parts = []
            for v in range(VARS):
                coef_v = coef_ref[v + 1, pl.ds(0, 8), :]
                coef_h = coef_ref[v + 1, pl.ds(8, 8), :]
                upper = places[LOWER + term * VARS + v]
                uppers.append(upper)
                parts.append(
                    weight_ref[term, pl.ds(v, 1), :]
                    * (coef_v * diff[upper, pl.ds(0, 8), :] + coef_h * diff[upper, pl.ds(8, 8), :])
                )
                gains.append(weight_ref[term, pl.ds(VARS + v, 1), :] * (coef_v * vert + coef_h * hori))
            while len(parts) > 1:
                parts = [x + y for x, y in zip(parts[::2], parts[1::2])] + parts[len(parts) // 2 * 2 :]
            mine.append(parts[0])
        for i, term in enumerate(terms):
            lower = places[term]
            total[lower] = total[lower] + mine[i]
            sums = [total[uppers[i * VARS + v]] + gains[i * VARS + v] for v in range(VARS)]
            for v in range(VARS):
                total[uppers[i * VARS + v]] = sums[v]
        return carry

    lax.fori_loop(0, LOWER // 6, couple, 0)

    def store(group, carry):
        made = []
        for p in range(PAIRS):
            a = total[group * (2 * PAIRS) + p]
            b = total[group * (2 * PAIRS) + PAIRS + p]
            made.append(jnp.where(low, a, b) + pltpu.roll(jnp.where(low, b, a), 64, 1))
        for p in range(PAIRS):
            out_ref[group, pl.ds(8 * p, 8), :] = made[p]
        return carry

    lax.fori_loop(0, groups, store, 0, unroll=8)


def unpack_kernel(got_ref, result_ref, out_ref, sem):
    low = lanes_of() < 64
    mask, _ = here()

    def send(r):
        rows = pl.ds(8 * r, 8)
        return pltpu.make_async_copy(out_ref.at[:, rows], result_ref.at[:, rows], sem.at[r])

    for r in range(4):
        for h in range(2):
            for p in range(PAIRS):
                one = got_ref[holder(r, 2 * h) ^ mask, pl.ds(8 * p, 8), :]
                two = got_ref[holder(r, 2 * h + 1) ^ mask, pl.ds(8 * p, 8), :]
                out_ref[p, pl.ds(8 * r, 8), pl.ds(128 * h, 128)] = jnp.where(
                    low, one, pltpu.roll(two, 64, 1)
                )
                out_ref[p + PAIRS, pl.ds(8 * r, 8), pl.ds(128 * h, 128)] = jnp.where(
                    low, pltpu.roll(one, 64, 1), two
                )
        send(r).start()
    for r in range(4):
        send(r).wait()


def vmem():
    return pl.BlockSpec(memory_space=pltpu.VMEM)


def hbm():
    return pl.BlockSpec(memory_space=pltpu.HBM)


def f32(*shape):
    return jax.ShapeDtypeStruct(shape, jnp.float32)


PARAMS = pltpu.CompilerParams(vmem_limit_bytes=32 * 1024 * 1024)


def cost(micros):
    return pl.CostEstimate(flops=0, bytes_accessed=micros * 3000000, transcendentals=0)


def pack(fields, groups):
    return pl.pallas_call(
        pack_kernel,
        out_shape=f32(groups, ROWS, 128),
        in_specs=[vmem()],
        out_specs=hbm(),
        scratch_shapes=[
            pltpu.VMEM((groups, ROWS, 128), jnp.float32),
            pltpu.SemaphoreType.DMA((groups,)),
        ],
        compiler_params=PARAMS,
        cost_estimate=cost(2),
    )(fields)


def edges(got):
    return pl.pallas_call(
        edge_kernel,
        out_shape=f32(got.shape[0] * PAIRS, 128),
        in_specs=[vmem()],
        out_specs=vmem(),
        compiler_params=PARAMS,
        cost_estimate=cost(1),
    )(got)


def coefs(modes, edge, weights):
    return pl.pallas_call(
        coef_kernel,
        out_shape=f32(modes.shape[0], 16, 128),
        in_specs=[vmem(), vmem(), hbm()],
        out_specs=vmem(),
        compiler_params=PARAMS,
        cost_estimate=cost(1),
    )(modes, edge, weights)


def load(own, got, coef):
    slots = got.shape[0] * 2 * PAIRS
    return pl.pallas_call(
        load_kernel,
        out_shape=(f32(slots, 16, 128), f32(slots, 8, 128)),
        in_specs=[vmem()] * 3,
        out_specs=(vmem(), vmem()),
        compiler_params=PARAMS,
        cost_estimate=cost(4),
    )(own, got, coef)


def mix(places, own, weights, diff, total, edge, coef):
    slots = diff.shape[0]
    return pl.pallas_call(
        mix_kernel,
        out_shape=f32(slots // (2 * PAIRS), BLOCK, 128),
        in_specs=[vmem()] * 7,
        out_specs=vmem(),
        scratch_shapes=[
            pltpu.VMEM((slots, 16, 128), jnp.float32),
            pltpu.VMEM((slots, 8, 128), jnp.float32),
            pltpu.SMEM(places.shape, jnp.int32),
            pltpu.SemaphoreType.DMA,
        ],
        compiler_params=PARAMS,
        cost_estimate=cost(5),
    )(places, own, weights, diff, total, edge, coef)


def unpack(got, shape):
    return pl.pallas_call(
        unpack_kernel,
        out_shape=f32(*shape),
        in_specs=[vmem()],
        out_specs=hbm(),
        scratch_shapes=[pltpu.VMEM(shape, jnp.float32), pltpu.SemaphoreType.DMA((4,))],
        compiler_params=PARAMS,
        cost_estimate=cost(1),
    )(got)


def tables(pair_list, pair_value, assign):
    terms = assign.shape[0]
    numbers = jnp.arange(terms, dtype=jnp.int32)
    row, col, mode = pair_list[:, 0:1], pair_list[:, 1:2], pair_list[:, 2:3]
    slot = jnp.sum(jnp.where(col == assign[None, :], numbers[None, :], 0), axis=1, keepdims=True)
    at = jnp.minimum(row, col) == numbers[None, :]
    kinds = jnp.arange(1 + 3 * VARS, dtype=jnp.int32)[None, :]
    wanted = jnp.where(kinds <= VARS, kinds, (kinds - 1) % VARS + 1)
    side = jnp.where(kinds <= VARS, row <= col, jnp.where(kinds <= 2 * VARS, row > col, row < col))
    value = jnp.where(kinds <= 2 * VARS, pair_value[:, None], slot.astype(jnp.float32))
    value = jnp.where((mode == wanted) & side, value, 0.0)
    found = lax.dot_general(
        at.astype(jnp.float32),
        value,
        (((0,), (0,)), ((), ())),
        precision=lax.Precision.HIGHEST,
        preferred_element_type=jnp.float32,
    )
    coupled = jnp.pad(found[:LOWER, 1 : 1 + 2 * VARS], ((0, 0), (0, 4)))
    uppers = jnp.round(found[:LOWER, 1 + 2 * VARS :]).astype(jnp.int32).reshape(-1)
    weights = jnp.broadcast_to(coupled[:, :, None], coupled.shape + (128,))
    held = assign[:, None] == numbers[None, :]
    own = jnp.sum(jnp.where(held, found[:, 0][None, :], 0.0), axis=1, keepdims=True)
    lowers = jnp.sum(jnp.where(held[:, :LOWER], numbers[:, None], 0), axis=0)
    return jnp.concatenate([lowers, uppers]), jnp.broadcast_to(own, (terms, 128)), weights


def shards(fields, modes, pair_list, pair_value, assign):
    groups = lax.axis_size("term")
    count = lax.axis_size("space")
    passes = []
    for c in range(groups // 4):
        for s in range(count - 1):
            lower = (holder(0, c) ^ mask_at(s + 1)) * count + s + 1
            upper = (holder(3, c) ^ mask_at(s)) * count + s
            passes += [(lower, upper), (upper, lower)]
    sent = pack(fields, groups)
    sent, modes = lax.optimization_barrier((sent, modes))
    got = lax.all_to_all(sent, "term", 0, 0, tiled=True)
    places, own, weights = tables(pair_list, pair_value, assign)
    _, place = here()
    edge = jnp.where(row_group(place) == 0, modes[:, 0], modes[:, modes.shape[1] - 1])
    coef = coefs(modes, lax.ppermute(edge, ("term", "space"), passes), weights)
    got, coef, places, own = lax.optimization_barrier((got, coef, places, own))
    beyond = lax.ppermute(edges(got), ("term", "space"), passes)
    diff, total = load(own, got, coef)
    mixed = mix(places, own, weights, diff, total, beyond, coef)
    back = lax.all_to_all(mixed, "term", 0, 0, tiled=True)
    return unpack(back, fields.shape)


def solution(mesh):
    return jax.shard_map(
        shards,
        mesh=mesh,
        in_specs=(P("term", "space", None), P(None, "space", None), P(), P(), P()),
        out_specs=P("term", "space", None),
        check_vma=False,
    )
```

```python
import jax
import jax.numpy as jnp
from jax import lax
from jax.experimental import pallas as pl
from jax.experimental.pallas import tpu as pltpu
from jax.sharding import PartitionSpec as P

PAIRS = 9
BLOCK = 8 * PAIRS
ROWS = 96
FIRST = 72
SECOND = 81
SIDE = 90
LOWER = 66
VARS = 10


def holder(r, c):
    return 4 * c + (r ^ c)


def rank(device):
    return (device & 1) << 3 | (device & 2) << 1 | (device & 4) >> 1 | (device >> 3 ^ 1)


def mask_at(space):
    return (space >> 1 & 1) * 8 + (space & 1) * 3


def here():
    mask = mask_at(lax.axis_index("space"))
    return mask, lax.axis_index("term") ^ mask


def row_group(place):
    return (place & 3) ^ (place >> 2)


def lanes_of(shape=(8, 128)):
    return lax.broadcasted_iota(jnp.int32, shape, 1)


def subs_of(shape=(8, 128)):
    return lax.broadcasted_iota(jnp.int32, shape, 0)


def pack_kernel(f_ref, sent_ref, out_ref, out_sem):
    lane = lanes_of()
    low = lane < 64
    even = lane % 2 == 0
    spare = lane % 64 >= 32
    mask, _ = here()

    def send(r, c):
        to = rank(holder(r, c) ^ mask)
        return pltpu.make_async_copy(out_ref.at[to], sent_ref.at[to], out_sem.at[4 * r + c])

    for r in range(4):
        near, far = [], []
        for h in range(2):
            ga = jnp.zeros((8, 128), jnp.float32)
            gb = jnp.zeros((8, 128), jnp.float32)
            for p in range(PAIRS):
                a = f_ref[p, pl.ds(8 * r, 8), pl.ds(128 * h, 128)]
                b = f_ref[p + PAIRS, pl.ds(8 * r, 8), pl.ds(128 * h, 128)]
                both = (
                    jnp.where(low, a, pltpu.roll(b, 64, 1)),
                    jnp.where(low, pltpu.roll(a, 64, 1), b),
                )
                for o in range(2):
                    c = 2 * h + o
                    first, last = both[o][0:1], both[o][7:8]
                    out_ref[rank(holder(r, c) ^ mask), pl.ds(8 * p, 8), :] = both[o]
                    if r == 0:
                        out_ref[rank(holder(0, c) ^ mask), pl.ds(FIRST + p, 1), :] = first
                    if r == 3:
                        out_ref[rank(holder(3, c) ^ mask), pl.ds(FIRST + p, 1), :] = last
                    if r < 3:
                        out_ref[rank(holder(r + 1, c) ^ mask), pl.ds((FIRST if r < 2 else SECOND) + p, 1), :] = last
                    if r > 0:
                        out_ref[rank(holder(r - 1, c) ^ mask), pl.ds(SECOND + p, 1), :] = first
                pair = (lane % 64) // 2 == p
                ga = jnp.where(pair, pltpu.roll(a, (2 * p - 63) % 128, 1), ga)
                gb = jnp.where(pair, pltpu.roll(b, 2 * p + 1, 1), gb)
            near.append(jnp.where(low, ga, gb))
            far.append(pltpu.roll(jnp.where(low, gb, ga), 64, 1))
        zero = jnp.zeros((8, 128), jnp.float32)
        sides = (
            jnp.where(even, zero, near[0]),
            jnp.where(even, near[0], far[1]),
            jnp.where(even, far[0], near[1]),
            jnp.where(even, near[1], zero),
        )
        for c in range(4):
            moved = pltpu.roll(pltpu.roll(sides[c], 32, 1), 2, 0)
            kept = jnp.where(spare, moved, sides[c])
            out_ref[rank(holder(r, c) ^ mask), pl.ds(SIDE, 6), :] = kept[0:6]
        for done in ((r - 1, r) if r == 3 else (r - 1,)):
            if done >= 0:
                for c in range(4):
                    send(done, c).start()
    for r in range(4):
        for c in range(4):
            send(r, c).wait()


def edge_kernel(got_ref, edge_ref):
    groups = got_ref.shape[0]
    for group in range(groups):
        edge_ref[pl.ds(8 * group, 8), :] = got_ref[group, pl.ds(FIRST, 8), :]
        edge_ref[pl.ds(8 * groups + group, 1), :] = got_ref[group, pl.ds(FIRST + 8, 1), :]


def coef_kernel(modes_ref, edge_ref, weight_ref, coef_ref):
    _, place = here()
    low = lanes_of() < 64
    block_row = row_group(place)
    block_col = place >> 2
    first = block_row == 0
    last = block_row == 3
    odd = block_col % 2 == 1
    right_half = block_col >= 2
    lane = lanes_of((8, 256))
    sub = subs_of((8, 256))
    for k in range(modes_ref.shape[0]):
        cells = modes_ref[k, pl.ds(pl.multiple_of(8 * block_row, 8), 8), :]
        before = modes_ref[k, pl.ds(pl.multiple_of(8 * jnp.maximum(block_row - 1, 0), 8), 8), :]
        after = modes_ref[k, pl.ds(pl.multiple_of(8 * jnp.minimum(block_row + 1, 3), 8), 8), :]
        over = jnp.where(first, edge_ref[pl.ds(k, 1), :], before[7:8])
        under = jnp.where(last, edge_ref[pl.ds(k, 1), :], after[0:1])
        up = jnp.where(sub == 0, over, pltpu.roll(cells, 1, 0))
        down = jnp.where(sub == 7, under, pltpu.roll(cells, 7, 0))
        left = jnp.where(lane == 0, 0.0, pltpu.roll(cells, 1, 1))
        right = jnp.where(lane == 255, 0.0, pltpu.roll(cells, 255, 1))

        def both(x, y):
            x = 0.5 * (cells + x)
            y = 0.5 * (cells + y)
            x = jnp.where(right_half, x[:, 128:], x[:, :128])
            y = jnp.where(right_half, y[:, 128:], y[:, :128])
            return jnp.where(
                odd,
                jnp.where(low, pltpu.roll(x, 64, 1), y),
                jnp.where(low, x, pltpu.roll(y, 64, 1)),
            )

        coef_ref[k, pl.ds(0, 8), :] = both(up, down)
        coef_ref[k, pl.ds(8, 8), :] = both(left, right)


def load_kernel(own_ref, got_ref, coef_ref, diff_ref, total_ref):
    _, place = here()
    lane, sub = lanes_of(), subs_of()
    low = lane < 64
    block_row = row_group(place)
    first = block_row == 0
    last = block_row == 3
    over_one = (sub == 0) & jnp.logical_not(first | last)
    over_two = (sub == 0) & last
    under = (sub == 7) & jnp.logical_not(last)
    inner_up = sub > 0
    inner_down = sub < 7

    def load(group, carry):
        tail = got_ref[group, pl.ds(ROWS - 8, 8), :]
        beside = jnp.where(
            sub < 6, pltpu.roll(tail, 6, 0), pltpu.roll(pltpu.roll(tail, 96, 1), 4, 0)
        )
        made = []
        for p in range(PAIRS):
            cells = got_ref[group, pl.ds(8 * p, 8), :]
            one = got_ref[group, pl.ds(FIRST + p, 1), :]
            two = got_ref[group, pl.ds(SECOND + p, 1), :]
            above = jnp.where(over_one, one, jnp.where(over_two, two, 0.0))
            below = jnp.where(under, two, 0.0)
            up = cells - jnp.where(inner_up, pltpu.roll(cells, 1, 0), above)
            down = cells - jnp.where(inner_down, pltpu.roll(cells, 7, 0), below)
            left = cells - jnp.where(
                lane % 64 == 0, pltpu.roll(beside, (128 - 2 * p) % 128, 1), pltpu.roll(cells, 1, 1)
            )
            right = cells - jnp.where(
                lane % 64 == 63, pltpu.roll(beside, 62 - 2 * p, 1), pltpu.roll(cells, 127, 1)
            )
            vert = pltpu.roll(jnp.where(low, down, up), 64, 1)
            hori = pltpu.roll(jnp.where(low, right, left), 64, 1)
            made.append((p, jnp.where(low, up, vert), jnp.where(low, left, hori)))
            made.append((p + PAIRS, jnp.where(low, vert, down), jnp.where(low, hori, right)))
        coef_v = coef_ref[0, pl.ds(0, 8), :]
        coef_h = coef_ref[0, pl.ds(8, 8), :]
        for i, vert, hori in made:
            slot = group * (2 * PAIRS) + i
            diff_ref[slot, pl.ds(0, 8), :] = vert
            diff_ref[slot, pl.ds(8, 8), :] = hori
            total_ref[slot] = own_ref[pl.ds(slot, 1), :] * (coef_v * vert + coef_h * hori)
        return carry

    lax.fori_loop(0, got_ref.shape[0], load, 0, unroll=2)


def mix_kernel(
    place_ref, own_ref, weight_ref, diff_ref, start_ref, edge_ref, coef_ref, out_ref, diff, total, places, sem
):
    copy = pltpu.make_async_copy(place_ref, places, sem)
    copy.start()
    _, place = here()
    lane, sub = lanes_of(), subs_of()
    low = lane < 64
    groups = out_ref.shape[0]
    first = row_group(place) == 0
    last = row_group(place) == 3
    meets = jnp.where((low & (sub == 0) & first) | ((lane >= 64) & (sub == 7) & last), 1.0, 0.0)

    def patch(group, carry):
        edge = edge_ref[pl.ds(pl.multiple_of(8 * group, 8), 8), :]
        more = edge_ref[pl.ds(8 * groups + group, 1), :]
        rows = []
        for part in (edge, more):
            turned = pltpu.roll(part, 64, 1)
            rows.append((jnp.where(first, part, turned), jnp.where(first, turned, part)))
        coef_v = coef_ref[0, pl.ds(0, 8), :]
        made = []
        for p in range(PAIRS):
            for o in range(2):
                slot = group * (2 * PAIRS) + o * PAIRS + p
                beyond = meets * (rows[0][o][p : p + 1] if p < 8 else rows[1][o])
                vert = diff_ref[slot, pl.ds(0, 8), :] - beyond
                hori = diff_ref[slot, pl.ds(8, 8), :]
                made.append((slot, vert, hori, start_ref[slot] - own_ref[pl.ds(slot, 1), :] * (coef_v * beyond)))
        for slot, vert, hori, value in made:
            diff[slot, pl.ds(0, 8), :] = vert
            diff[slot, pl.ds(8, 8), :] = hori
            total[slot] = value
        return carry

    lax.fori_loop(0, groups, patch, 0, unroll=4)
    copy.wait()

    def couple(step, carry):
        terms = [6 * step + i for i in range(6)]
        uppers, gains, mine = [], [], []
        for term in terms:
            lower = places[term]
            vert = diff[lower, pl.ds(0, 8), :]
            hori = diff[lower, pl.ds(8, 8), :]
            parts = []
            for v in range(VARS):
                coef_v = coef_ref[v + 1, pl.ds(0, 8), :]
                coef_h = coef_ref[v + 1, pl.ds(8, 8), :]
                upper = places[LOWER + term * VARS + v]
                uppers.append(upper)
                parts.append(
                    weight_ref[term, pl.ds(v, 1), :]
                    * (coef_v * diff[upper, pl.ds(0, 8), :] + coef_h * diff[upper, pl.ds(8, 8), :])
                )
                gains.append(weight_ref[term, pl.ds(VARS + v, 1), :] * (coef_v * vert + coef_h * hori))
            while len(parts) > 1:
                parts = [x + y for x, y in zip(parts[::2], parts[1::2])] + parts[len(parts) // 2 * 2 :]
            mine.append(parts[0])
        for i, term in enumerate(terms):
            lower = places[term]
            total[lower] = total[lower] + mine[i]
            sums = [total[uppers[i * VARS + v]] + gains[i * VARS + v] for v in range(VARS)]
            for v in range(VARS):
                total[uppers[i * VARS + v]] = sums[v]
        return carry

    lax.fori_loop(0, LOWER // 6, couple, 0)

    def store(group, carry):
        made = []
        for p in range(PAIRS):
            a = total[group * (2 * PAIRS) + p]
            b = total[group * (2 * PAIRS) + PAIRS + p]
            made.append(jnp.where(low, a, b) + pltpu.roll(jnp.where(low, b, a), 64, 1))
        for p in range(PAIRS):
            out_ref[group, pl.ds(8 * p, 8), :] = made[p]
        return carry

    lax.fori_loop(0, groups, store, 0, unroll=8)


def unpack_kernel(got_ref, result_ref, out_ref, sem):
    low = lanes_of() < 64
    mask, _ = here()

    def send(r):
        rows = pl.ds(8 * r, 8)
        return pltpu.make_async_copy(out_ref.at[:, rows], result_ref.at[:, rows], sem.at[r])

    for r in range(4):
        for h in range(2):
            for p in range(PAIRS):
                one = got_ref[rank(holder(r, 2 * h) ^ mask), pl.ds(8 * p, 8), :]
                two = got_ref[rank(holder(r, 2 * h + 1) ^ mask), pl.ds(8 * p, 8), :]
                out_ref[p, pl.ds(8 * r, 8), pl.ds(128 * h, 128)] = jnp.where(
                    low, one, pltpu.roll(two, 64, 1)
                )
                out_ref[p + PAIRS, pl.ds(8 * r, 8), pl.ds(128 * h, 128)] = jnp.where(
                    low, pltpu.roll(one, 64, 1), two
                )
        send(r).start()
    for r in range(4):
        send(r).wait()


def vmem():
    return pl.BlockSpec(memory_space=pltpu.VMEM)


def hbm():
    return pl.BlockSpec(memory_space=pltpu.HBM)


def f32(*shape):
    return jax.ShapeDtypeStruct(shape, jnp.float32)


PARAMS = pltpu.CompilerParams(vmem_limit_bytes=32 * 1024 * 1024)


def cost(micros):
    return pl.CostEstimate(flops=0, bytes_accessed=micros * 3000000, transcendentals=0)


def pack(fields, groups):
    return pl.pallas_call(
        pack_kernel,
        out_shape=f32(groups, ROWS, 128),
        in_specs=[vmem()],
        out_specs=hbm(),
        scratch_shapes=[
            pltpu.VMEM((groups, ROWS, 128), jnp.float32),
            pltpu.SemaphoreType.DMA((groups,)),
        ],
        compiler_params=PARAMS,
        cost_estimate=cost(2),
    )(fields)


def edges(got):
    return pl.pallas_call(
        edge_kernel,
        out_shape=f32(got.shape[0] * PAIRS, 128),
        in_specs=[vmem()],
        out_specs=vmem(),
        compiler_params=PARAMS,
        cost_estimate=cost(1),
    )(got)


def coefs(modes, edge, weights):
    return pl.pallas_call(
        coef_kernel,
        out_shape=f32(modes.shape[0], 16, 128),
        in_specs=[vmem(), vmem(), hbm()],
        out_specs=vmem(),
        compiler_params=PARAMS,
        cost_estimate=cost(1),
    )(modes, edge, weights)


def load(own, got, coef):
    slots = got.shape[0] * 2 * PAIRS
    return pl.pallas_call(
        load_kernel,
        out_shape=(f32(slots, 16, 128), f32(slots, 8, 128)),
        in_specs=[vmem()] * 3,
        out_specs=(vmem(), vmem()),
        compiler_params=PARAMS,
        cost_estimate=cost(4),
    )(own, got, coef)


def mix(places, own, weights, diff, total, edge, coef):
    slots = diff.shape[0]
    return pl.pallas_call(
        mix_kernel,
        out_shape=f32(slots // (2 * PAIRS), BLOCK, 128),
        in_specs=[vmem()] * 7,
        out_specs=vmem(),
        scratch_shapes=[
            pltpu.VMEM((slots, 16, 128), jnp.float32),
            pltpu.VMEM((slots, 8, 128), jnp.float32),
            pltpu.SMEM(places.shape, jnp.int32),
            pltpu.SemaphoreType.DMA,
        ],
        compiler_params=PARAMS,
        cost_estimate=cost(5),
    )(places, own, weights, diff, total, edge, coef)


def unpack(got, shape):
    return pl.pallas_call(
        unpack_kernel,
        out_shape=f32(*shape),
        in_specs=[vmem()],
        out_specs=hbm(),
        scratch_shapes=[pltpu.VMEM(shape, jnp.float32), pltpu.SemaphoreType.DMA((4,))],
        compiler_params=PARAMS,
        cost_estimate=cost(1),
    )(got)


def tables(pair_list, pair_value, assign):
    terms = assign.shape[0]
    numbers = jnp.arange(terms, dtype=jnp.int32)
    row, col, mode = pair_list[:, 0:1], pair_list[:, 1:2], pair_list[:, 2:3]
    slot = jnp.sum(jnp.where(col == assign[None, :], numbers[None, :], 0), axis=1, keepdims=True)
    at = jnp.minimum(row, col) == numbers[None, :]
    kinds = jnp.arange(1 + 3 * VARS, dtype=jnp.int32)[None, :]
    wanted = jnp.where(kinds <= VARS, kinds, (kinds - 1) % VARS + 1)
    side = jnp.where(kinds <= VARS, row <= col, jnp.where(kinds <= 2 * VARS, row > col, row < col))
    value = jnp.where(kinds <= 2 * VARS, pair_value[:, None], slot.astype(jnp.float32))
    value = jnp.where((mode == wanted) & side, value, 0.0)
    found = lax.dot_general(
        at.astype(jnp.float32),
        value,
        (((0,), (0,)), ((), ())),
        precision=lax.Precision.HIGHEST,
        preferred_element_type=jnp.float32,
    )
    coupled = jnp.pad(found[:LOWER, 1 : 1 + 2 * VARS], ((0, 0), (0, 4)))
    uppers = jnp.round(found[:LOWER, 1 + 2 * VARS :]).astype(jnp.int32).reshape(-1)
    weights = jnp.broadcast_to(coupled[:, :, None], coupled.shape + (128,))
    held = assign[:, None] == numbers[None, :]
    own = jnp.sum(jnp.where(held, found[:, 0][None, :], 0.0), axis=1, keepdims=True)
    lowers = jnp.sum(jnp.where(held[:, :LOWER], numbers[:, None], 0), axis=0)
    places = jnp.pad(jnp.concatenate([lowers, uppers]), (0, 1024 - LOWER * (1 + VARS)))
    return places, jnp.broadcast_to(own, (terms, 128)), weights


def shards(fields, modes, pair_list, pair_value, assign):
    groups = lax.axis_size("term")
    count = lax.axis_size("space")
    passes = []
    for c in range(groups // 4):
        for s in range(count - 1):
            lower = (holder(0, c) ^ mask_at(s + 1)) * count + s + 1
            upper = (holder(3, c) ^ mask_at(s)) * count + s
            passes += [(lower, upper), (upper, lower)]
    order = sorted(range(groups), key=rank)
    assign = assign.reshape(groups, -1)[jnp.array(order)].reshape(-1)
    sent = pack(fields, groups)
    sent, modes = lax.optimization_barrier((sent, modes))
    got = lax.all_to_all(sent, "term", 0, 0, axis_index_groups=[order], tiled=True)
    places, own, weights = tables(pair_list, pair_value, assign)
    _, place = here()
    edge = jnp.where(row_group(place) == 0, modes[:, 0], modes[:, modes.shape[1] - 1])
    coef = coefs(modes, lax.ppermute(edge, ("term", "space"), passes), weights)
    got, coef, places, own = lax.optimization_barrier((got, coef, places, own))
    beyond = lax.ppermute(edges(got), ("term", "space"), passes)
    diff, total = load(own, got, coef)
    mixed = mix(places, own, weights, diff, total, beyond, coef)
    back = lax.all_to_all(mixed, "term", 0, 0, axis_index_groups=[order], tiled=True)
    return unpack(back, fields.shape)


def solution(mesh):
    return jax.shard_map(
        shards,
        mesh=mesh,
        in_specs=(P("term", "space", None), P(None, "space", None), P(), P(), P()),
        out_specs=P("term", "space", None),
        check_vma=False,
    )
```

```python
import jax
import jax.numpy as jnp
from jax import lax
from jax.experimental import pallas as pl
from jax.experimental.pallas import tpu as pltpu
from jax.sharding import PartitionSpec as P

PAIRS = 9
BLOCK = 8 * PAIRS
ROWS = 88
HALO = 72
SIDE = 81
LOWER = 66
VARS = 10


def holder(r, c):
    return 4 * c + (r ^ c)


def rank(device):
    return (device & 1) << 3 | (device & 2) << 1 | (device & 4) >> 1 | (device >> 3 ^ 1)


def mask_at(space):
    return (space >> 1 & 1) * 8 + (space & 1) * 3


def here():
    mask = mask_at(lax.axis_index("space"))
    return mask, lax.axis_index("term") ^ mask


def row_group(place):
    return (place & 3) ^ (place >> 2)


def lanes_of(shape=(8, 128)):
    return lax.broadcasted_iota(jnp.int32, shape, 1)


def subs_of(shape=(8, 128)):
    return lax.broadcasted_iota(jnp.int32, shape, 0)


def pack_kernel(f_ref, sent_ref, out_ref, out_sem):
    lane = lanes_of()
    low = lane < 64
    even = lane % 2 == 0
    spare = lane % 64 >= 32
    mask, _ = here()

    def send(r, c):
        to = rank(holder(r, c) ^ mask)
        return pltpu.make_async_copy(out_ref.at[to], sent_ref.at[to], out_sem.at[4 * r + c])

    for r in range(4):
        near, far = [], []
        for h in range(2):
            ga = jnp.zeros((8, 128), jnp.float32)
            gb = jnp.zeros((8, 128), jnp.float32)
            for p in range(PAIRS):
                a = f_ref[p, pl.ds(8 * r, 8), pl.ds(128 * h, 128)]
                b = f_ref[p + PAIRS, pl.ds(8 * r, 8), pl.ds(128 * h, 128)]
                both = (
                    jnp.where(low, a, pltpu.roll(b, 64, 1)),
                    jnp.where(low, pltpu.roll(a, 64, 1), b),
                )
                for o in range(2):
                    c = 2 * h + o
                    first, last = both[o][0:1], both[o][7:8]
                    out_ref[rank(holder(r, c) ^ mask), pl.ds(8 * p, 8), :] = both[o]
                    if r % 2 == 0:
                        out_ref[rank(holder(r + 1, c) ^ mask), pl.ds(HALO + p, 1), :] = last
                    else:
                        out_ref[rank(holder(r - 1, c) ^ mask), pl.ds(HALO + p, 1), :] = first
                pair = (lane % 64) // 2 == p
                ga = jnp.where(pair, pltpu.roll(a, (2 * p - 63) % 128, 1), ga)
                gb = jnp.where(pair, pltpu.roll(b, 2 * p + 1, 1), gb)
            near.append(jnp.where(low, ga, gb))
            far.append(pltpu.roll(jnp.where(low, gb, ga), 64, 1))
        zero = jnp.zeros((8, 128), jnp.float32)
        sides = (
            jnp.where(even, zero, near[0]),
            jnp.where(even, near[0], far[1]),
            jnp.where(even, far[0], near[1]),
            jnp.where(even, near[1], zero),
        )
        for c in range(4):
            moved = pltpu.roll(pltpu.roll(sides[c], 32, 1), 2, 0)
            kept = jnp.where(spare, moved, sides[c])
            out_ref[rank(holder(r, c) ^ mask), pl.ds(SIDE, 7), :] = kept[0:7]
        for done in (r - 1, r):
            if r % 2 == 1:
                for c in range(4):
                    send(done, c).start()
    for r in range(4):
        for c in range(4):
            send(r, c).wait()


def edge_kernel(got_ref, edge_ref):
    _, place = here()
    groups = got_ref.shape[0]
    even = row_group(place) % 2 == 0
    for row, wanted in ((0, even), (7, jnp.logical_not(even))):

        @pl.when(wanted)
        def _():
            for group in range(groups):
                edge_ref[pl.ds(8 * group, 8), :] = got_ref[group, pl.ds(row, 8, stride=8), :]
                edge_ref[pl.ds(8 * groups + group, 1), :] = got_ref[group, pl.ds(64 + row, 1), :]


def coef_kernel(modes_ref, edge_ref, weight_ref, coef_ref):
    _, place = here()
    low = lanes_of() < 64
    block_row = row_group(place)
    block_col = place >> 2
    first = block_row == 0
    last = block_row == 3
    odd = block_col % 2 == 1
    right_half = block_col >= 2
    lane = lanes_of((8, 256))
    sub = subs_of((8, 256))
    for k in range(modes_ref.shape[0]):
        cells = modes_ref[k, pl.ds(pl.multiple_of(8 * block_row, 8), 8), :]
        before = modes_ref[k, pl.ds(pl.multiple_of(8 * jnp.maximum(block_row - 1, 0), 8), 8), :]
        after = modes_ref[k, pl.ds(pl.multiple_of(8 * jnp.minimum(block_row + 1, 3), 8), 8), :]
        over = jnp.where(first, edge_ref[pl.ds(k, 1), :], before[7:8])
        under = jnp.where(last, edge_ref[pl.ds(k, 1), :], after[0:1])
        up = jnp.where(sub == 0, over, pltpu.roll(cells, 1, 0))
        down = jnp.where(sub == 7, under, pltpu.roll(cells, 7, 0))
        left = jnp.where(lane == 0, 0.0, pltpu.roll(cells, 1, 1))
        right = jnp.where(lane == 255, 0.0, pltpu.roll(cells, 255, 1))

        def both(x, y):
            x = 0.5 * (cells + x)
            y = 0.5 * (cells + y)
            x = jnp.where(right_half, x[:, 128:], x[:, :128])
            y = jnp.where(right_half, y[:, 128:], y[:, :128])
            return jnp.where(
                odd,
                jnp.where(low, pltpu.roll(x, 64, 1), y),
                jnp.where(low, x, pltpu.roll(y, 64, 1)),
            )

        coef_ref[k, pl.ds(0, 8), :] = both(up, down)
        coef_ref[k, pl.ds(8, 8), :] = both(left, right)


def load_kernel(own_ref, got_ref, coef_ref, diff_ref, total_ref):
    _, place = here()
    lane, sub = lanes_of(), subs_of()
    low = lane < 64
    even = row_group(place) % 2 == 0
    over = (sub == 0) & jnp.logical_not(even)
    under = (sub == 7) & even
    inner_up = sub > 0
    inner_down = sub < 7

    def load(group, carry):
        tail = got_ref[group, pl.ds(ROWS - 8, 8), :]
        beside = jnp.where(
            sub < 6, pltpu.roll(tail, 7, 0), pltpu.roll(pltpu.roll(tail, 96, 1), 5, 0)
        )
        made = []
        for p in range(PAIRS):
            cells = got_ref[group, pl.ds(8 * p, 8), :]
            halo = got_ref[group, pl.ds(HALO + p, 1), :]
            above = jnp.where(over, halo, 0.0)
            below = jnp.where(under, halo, 0.0)
            up = cells - jnp.where(inner_up, pltpu.roll(cells, 1, 0), above)
            down = cells - jnp.where(inner_down, pltpu.roll(cells, 7, 0), below)
            left = cells - jnp.where(
                lane % 64 == 0, pltpu.roll(beside, (128 - 2 * p) % 128, 1), pltpu.roll(cells, 1, 1)
            )
            right = cells - jnp.where(
                lane % 64 == 63, pltpu.roll(beside, 62 - 2 * p, 1), pltpu.roll(cells, 127, 1)
            )
            vert = pltpu.roll(jnp.where(low, down, up), 64, 1)
            hori = pltpu.roll(jnp.where(low, right, left), 64, 1)
            made.append((p, jnp.where(low, up, vert), jnp.where(low, left, hori)))
            made.append((p + PAIRS, jnp.where(low, vert, down), jnp.where(low, hori, right)))
        coef_v = coef_ref[0, pl.ds(0, 8), :]
        coef_h = coef_ref[0, pl.ds(8, 8), :]
        for i, vert, hori in made:
            slot = group * (2 * PAIRS) + i
            diff_ref[slot, pl.ds(0, 8), :] = vert
            diff_ref[slot, pl.ds(8, 8), :] = hori
            total_ref[slot] = own_ref[pl.ds(slot, 1), :] * (coef_v * vert + coef_h * hori)
        return carry

    lax.fori_loop(0, got_ref.shape[0], load, 0, unroll=2)


def mix_kernel(
    place_ref, own_ref, weight_ref, diff_ref, start_ref, edge_ref, coef_ref, out_ref, diff, total, places, sem
):
    copy = pltpu.make_async_copy(place_ref, places, sem)
    copy.start()
    _, place = here()
    lane, sub = lanes_of(), subs_of()
    low = lane < 64
    groups = out_ref.shape[0]
    even = row_group(place) % 2 == 0
    meets = jnp.where(
        (low & (sub == 0) & even) | ((lane >= 64) & (sub == 7) & jnp.logical_not(even)), 1.0, 0.0
    )

    def patch(group, carry):
        edge = edge_ref[pl.ds(pl.multiple_of(8 * group, 8), 8), :]
        more = edge_ref[pl.ds(8 * groups + group, 1), :]
        rows = []
        for part in (edge, more):
            turned = pltpu.roll(part, 64, 1)
            rows.append((jnp.where(even, part, turned), jnp.where(even, turned, part)))
        coef_v = coef_ref[0, pl.ds(0, 8), :]
        made = []
        for p in range(PAIRS):
            for o in range(2):
                slot = group * (2 * PAIRS) + o * PAIRS + p
                beyond = meets * (rows[0][o][p : p + 1] if p < 8 else rows[1][o])
                vert = diff_ref[slot, pl.ds(0, 8), :] - beyond
                hori = diff_ref[slot, pl.ds(8, 8), :]
                made.append((slot, vert, hori, start_ref[slot] - own_ref[pl.ds(slot, 1), :] * (coef_v * beyond)))
        for slot, vert, hori, value in made:
            diff[slot, pl.ds(0, 8), :] = vert
            diff[slot, pl.ds(8, 8), :] = hori
            total[slot] = value
        return carry

    lax.fori_loop(0, groups, patch, 0, unroll=4)
    copy.wait()

    def couple(step, carry):
        terms = [6 * step + i for i in range(6)]
        uppers, gains, mine = [], [], []
        for term in terms:
            lower = places[term]
            vert = diff[lower, pl.ds(0, 8), :]
            hori = diff[lower, pl.ds(8, 8), :]
            parts = []
            for v in range(VARS):
                coef_v = coef_ref[v + 1, pl.ds(0, 8), :]
                coef_h = coef_ref[v + 1, pl.ds(8, 8), :]
                upper = places[LOWER + term * VARS + v]
                uppers.append(upper)
                parts.append(
                    weight_ref[term, pl.ds(v, 1), :]
                    * (coef_v * diff[upper, pl.ds(0, 8), :] + coef_h * diff[upper, pl.ds(8, 8), :])
                )
                gains.append(weight_ref[term, pl.ds(VARS + v, 1), :] * (coef_v * vert + coef_h * hori))
            while len(parts) > 1:
                parts = [x + y for x, y in zip(parts[::2], parts[1::2])] + parts[len(parts) // 2 * 2 :]
            mine.append(parts[0])
        for i, term in enumerate(terms):
            lower = places[term]
            total[lower] = total[lower] + mine[i]
            sums = [total[uppers[i * VARS + v]] + gains[i * VARS + v] for v in range(VARS)]
            for v in range(VARS):
                total[uppers[i * VARS + v]] = sums[v]
        return carry

    lax.fori_loop(0, LOWER // 6, couple, 0)

    def store(group, carry):
        made = []
        for p in range(PAIRS):
            a = total[group * (2 * PAIRS) + p]
            b = total[group * (2 * PAIRS) + PAIRS + p]
            made.append(jnp.where(low, a, b) + pltpu.roll(jnp.where(low, b, a), 64, 1))
        for p in range(PAIRS):
            out_ref[group, pl.ds(8 * p, 8), :] = made[p]
        return carry

    lax.fori_loop(0, groups, store, 0, unroll=8)


def unpack_kernel(got_ref, result_ref, out_ref, sem):
    low = lanes_of() < 64
    mask, _ = here()

    def send(r):
        rows = pl.ds(8 * r, 8)
        return pltpu.make_async_copy(out_ref.at[:, rows], result_ref.at[:, rows], sem.at[r])

    for r in range(4):
        for h in range(2):
            for p in range(PAIRS):
                one = got_ref[rank(holder(r, 2 * h) ^ mask), pl.ds(8 * p, 8), :]
                two = got_ref[rank(holder(r, 2 * h + 1) ^ mask), pl.ds(8 * p, 8), :]
                out_ref[p, pl.ds(8 * r, 8), pl.ds(128 * h, 128)] = jnp.where(
                    low, one, pltpu.roll(two, 64, 1)
                )
                out_ref[p + PAIRS, pl.ds(8 * r, 8), pl.ds(128 * h, 128)] = jnp.where(
                    low, pltpu.roll(one, 64, 1), two
                )
        send(r).start()
    for r in range(4):
        send(r).wait()


def vmem():
    return pl.BlockSpec(memory_space=pltpu.VMEM)


def hbm():
    return pl.BlockSpec(memory_space=pltpu.HBM)


def f32(*shape):
    return jax.ShapeDtypeStruct(shape, jnp.float32)


PARAMS = pltpu.CompilerParams(vmem_limit_bytes=32 * 1024 * 1024)


def cost(micros):
    return pl.CostEstimate(flops=0, bytes_accessed=micros * 3000000, transcendentals=0)


def pack(fields, groups):
    return pl.pallas_call(
        pack_kernel,
        out_shape=f32(groups, ROWS, 128),
        in_specs=[vmem()],
        out_specs=hbm(),
        scratch_shapes=[
            pltpu.VMEM((groups, ROWS, 128), jnp.float32),
            pltpu.SemaphoreType.DMA((groups,)),
        ],
        compiler_params=PARAMS,
        cost_estimate=cost(2),
    )(fields)


def edges(got):
    return pl.pallas_call(
        edge_kernel,
        out_shape=f32(got.shape[0] * PAIRS, 128),
        in_specs=[vmem()],
        out_specs=vmem(),
        compiler_params=PARAMS,
        cost_estimate=cost(1),
    )(got)


def coefs(modes, edge, weights):
    return pl.pallas_call(
        coef_kernel,
        out_shape=f32(modes.shape[0], 16, 128),
        in_specs=[vmem(), vmem(), hbm()],
        out_specs=vmem(),
        compiler_params=PARAMS,
        cost_estimate=cost(1),
    )(modes, edge, weights)


def load(own, got, coef):
    slots = got.shape[0] * 2 * PAIRS
    return pl.pallas_call(
        load_kernel,
        out_shape=(f32(slots, 16, 128), f32(slots, 8, 128)),
        in_specs=[vmem()] * 3,
        out_specs=(vmem(), vmem()),
        compiler_params=PARAMS,
        cost_estimate=cost(4),
    )(own, got, coef)


def mix(places, own, weights, diff, total, edge, coef):
    slots = diff.shape[0]
    return pl.pallas_call(
        mix_kernel,
        out_shape=f32(slots // (2 * PAIRS), BLOCK, 128),
        in_specs=[vmem()] * 7,
        out_specs=vmem(),
        scratch_shapes=[
            pltpu.VMEM((slots, 16, 128), jnp.float32),
            pltpu.VMEM((slots, 8, 128), jnp.float32),
            pltpu.SMEM(places.shape, jnp.int32),
            pltpu.SemaphoreType.DMA,
        ],
        compiler_params=PARAMS,
        cost_estimate=cost(5),
    )(places, own, weights, diff, total, edge, coef)


def unpack(got, shape):
    return pl.pallas_call(
        unpack_kernel,
        out_shape=f32(*shape),
        in_specs=[vmem()],
        out_specs=hbm(),
        scratch_shapes=[pltpu.VMEM(shape, jnp.float32), pltpu.SemaphoreType.DMA((4,))],
        compiler_params=PARAMS,
        cost_estimate=cost(1),
    )(got)


def tables(pair_list, pair_value, assign):
    terms = assign.shape[0]
    numbers = jnp.arange(terms, dtype=jnp.int32)
    row, col, mode = pair_list[:, 0:1], pair_list[:, 1:2], pair_list[:, 2:3]
    slot = jnp.sum(jnp.where(col == assign[None, :], numbers[None, :], 0), axis=1, keepdims=True)
    at = jnp.minimum(row, col) == numbers[None, :]
    kinds = jnp.arange(1 + 3 * VARS, dtype=jnp.int32)[None, :]
    wanted = jnp.where(kinds <= VARS, kinds, (kinds - 1) % VARS + 1)
    side = jnp.where(kinds <= VARS, row <= col, jnp.where(kinds <= 2 * VARS, row > col, row < col))
    value = jnp.where(kinds <= 2 * VARS, pair_value[:, None], slot.astype(jnp.float32))
    value = jnp.where((mode == wanted) & side, value, 0.0)
    found = lax.dot_general(
        at.astype(jnp.float32),
        value,
        (((0,), (0,)), ((), ())),
        precision=lax.Precision.HIGHEST,
        preferred_element_type=jnp.float32,
    )
    coupled = jnp.pad(found[:LOWER, 1 : 1 + 2 * VARS], ((0, 0), (0, 4)))
    uppers = jnp.round(found[:LOWER, 1 + 2 * VARS :]).astype(jnp.int32).reshape(-1)
    weights = jnp.broadcast_to(coupled[:, :, None], coupled.shape + (128,))
    held = assign[:, None] == numbers[None, :]
    own = jnp.sum(jnp.where(held, found[:, 0][None, :], 0.0), axis=1, keepdims=True)
    lowers = jnp.sum(jnp.where(held[:, :LOWER], numbers[:, None], 0), axis=0)
    places = jnp.pad(jnp.concatenate([lowers, uppers]), (0, 1024 - LOWER * (1 + VARS)))
    return places, jnp.broadcast_to(own, (terms, 128)), weights


def shards(fields, modes, pair_list, pair_value, assign):
    groups = lax.axis_size("term")
    count = lax.axis_size("space")
    passes, between = [], []
    for c in range(groups // 4):
        for s in range(count):
            one, two = ((holder(r, c) ^ mask_at(s)) * count + s for r in (1, 2))
            between += [(one, two), (two, one)]
        for s in range(count - 1):
            lower = (holder(0, c) ^ mask_at(s + 1)) * count + s + 1
            upper = (holder(3, c) ^ mask_at(s)) * count + s
            passes += [(lower, upper), (upper, lower)]
    order = sorted(range(groups), key=rank)
    assign = assign.reshape(groups, -1)[jnp.array(order)].reshape(-1)
    sent = pack(fields, groups)
    sent, modes = lax.optimization_barrier((sent, modes))
    got = lax.all_to_all(sent, "term", 0, 0, axis_index_groups=[order], tiled=True)
    places, own, weights = tables(pair_list, pair_value, assign)
    _, place = here()
    edge = jnp.where(row_group(place) == 0, modes[:, 0], modes[:, modes.shape[1] - 1])
    coef = coefs(modes, lax.ppermute(edge, ("term", "space"), passes), weights)
    got, coef, places, own = lax.optimization_barrier((got, coef, places, own))
    beyond = lax.ppermute(edges(got), ("term", "space"), passes + between)
    diff, total = load(own, got, coef)
    mixed = mix(places, own, weights, diff, total, beyond, coef)
    back = lax.all_to_all(mixed, "term", 0, 0, axis_index_groups=[order], tiled=True)
    return unpack(back, fields.shape)


def solution(mesh):
    return jax.shard_map(
        shards,
        mesh=mesh,
        in_specs=(P("term", "space", None), P(None, "space", None), P(), P(), P()),
        out_specs=P("term", "space", None),
        check_vma=False,
    )
```

```python
import jax
import jax.numpy as jnp
from jax import lax
from jax.experimental import pallas as pl
from jax.experimental.pallas import tpu as pltpu
from jax.sharding import PartitionSpec as P

PAIRS = 9
BLOCK = 8 * PAIRS
ROWS = 88
HALO = 72
SIDE = 81
LOWER = 66
VARS = 10


def holder(r, c):
    return 4 * c + (r ^ c)


def rank(device):
    device = device ^ 15
    return (device & 1) << 3 | (device & 2) << 1 | (device & 4) >> 1 | (device >> 3 ^ 1)


def mask_at(space):
    return (space >> 1 & 1) * 8 + (space & 1) * 3


def here():
    mask = mask_at(lax.axis_index("space"))
    return mask, lax.axis_index("term") ^ mask


def row_group(place):
    return (place & 3) ^ (place >> 2)


def lanes_of(shape=(8, 128)):
    return lax.broadcasted_iota(jnp.int32, shape, 1)


def subs_of(shape=(8, 128)):
    return lax.broadcasted_iota(jnp.int32, shape, 0)


def pack_kernel(f_ref, sent_ref, out_ref, out_sem):
    lane = lanes_of()
    low = lane < 64
    even = lane % 2 == 0
    spare = lane % 64 >= 32
    mask, _ = here()

    def send(r, c):
        to = rank(holder(r, c) ^ mask)
        return pltpu.make_async_copy(out_ref.at[to], sent_ref.at[to], out_sem.at[4 * r + c])

    for r in range(4):
        near, far = [], []
        for h in range(2):
            ga = jnp.zeros((8, 128), jnp.float32)
            gb = jnp.zeros((8, 128), jnp.float32)
            for p in range(PAIRS):
                a = f_ref[p, pl.ds(8 * r, 8), pl.ds(128 * h, 128)]
                b = f_ref[p + PAIRS, pl.ds(8 * r, 8), pl.ds(128 * h, 128)]
                both = (
                    jnp.where(low, a, pltpu.roll(b, 64, 1)),
                    jnp.where(low, pltpu.roll(a, 64, 1), b),
                )
                for o in range(2):
                    c = 2 * h + o
                    first, last = both[o][0:1], both[o][7:8]
                    out_ref[rank(holder(r, c) ^ mask), pl.ds(8 * p, 8), :] = both[o]
                    if r % 2 == 0:
                        out_ref[rank(holder(r + 1, c) ^ mask), pl.ds(HALO + p, 1), :] = last
                    else:
                        out_ref[rank(holder(r - 1, c) ^ mask), pl.ds(HALO + p, 1), :] = first
                pair = (lane % 64) // 2 == p
                ga = jnp.where(pair, pltpu.roll(a, (2 * p - 63) % 128, 1), ga)
                gb = jnp.where(pair, pltpu.roll(b, 2 * p + 1, 1), gb)
            near.append(jnp.where(low, ga, gb))
            far.append(pltpu.roll(jnp.where(low, gb, ga), 64, 1))
        zero = jnp.zeros((8, 128), jnp.float32)
        sides = (
            jnp.where(even, zero, near[0]),
            jnp.where(even, near[0], far[1]),
            jnp.where(even, far[0], near[1]),
            jnp.where(even, near[1], zero),
        )
        for c in range(4):
            moved = pltpu.roll(pltpu.roll(sides[c], 32, 1), 2, 0)
            kept = jnp.where(spare, moved, sides[c])
            out_ref[rank(holder(r, c) ^ mask), pl.ds(SIDE, 7), :] = kept[0:7]
        for done in (r - 1, r):
            if r % 2 == 1:
                for c in range(4):
                    send(done, c).start()
    for r in range(4):
        for c in range(4):
            send(r, c).wait()


def edge_kernel(got_ref, edge_ref):
    _, place = here()
    groups = got_ref.shape[0]
    even = row_group(place) % 2 == 0
    for row, wanted in ((0, even), (7, jnp.logical_not(even))):

        @pl.when(wanted)
        def _():
            for group in range(groups):
                edge_ref[pl.ds(8 * group, 8), :] = got_ref[group, pl.ds(row, 8, stride=8), :]
                edge_ref[pl.ds(8 * groups + group, 1), :] = got_ref[group, pl.ds(64 + row, 1), :]


def coef_kernel(modes_ref, edge_ref, weight_ref, coef_ref):
    _, place = here()
    low = lanes_of() < 64
    block_row = row_group(place)
    block_col = place >> 2
    first = block_row == 0
    last = block_row == 3
    odd = block_col % 2 == 1
    right_half = block_col >= 2
    lane = lanes_of((8, 256))
    sub = subs_of((8, 256))
    for k in range(modes_ref.shape[0]):
        cells = modes_ref[k, pl.ds(pl.multiple_of(8 * block_row, 8), 8), :]
        before = modes_ref[k, pl.ds(pl.multiple_of(8 * jnp.maximum(block_row - 1, 0), 8), 8), :]
        after = modes_ref[k, pl.ds(pl.multiple_of(8 * jnp.minimum(block_row + 1, 3), 8), 8), :]
        over = jnp.where(first, edge_ref[pl.ds(k, 1), :], before[7:8])
        under = jnp.where(last, edge_ref[pl.ds(k, 1), :], after[0:1])
        up = jnp.where(sub == 0, over, pltpu.roll(cells, 1, 0))
        down = jnp.where(sub == 7, under, pltpu.roll(cells, 7, 0))
        left = jnp.where(lane == 0, 0.0, pltpu.roll(cells, 1, 1))
        right = jnp.where(lane == 255, 0.0, pltpu.roll(cells, 255, 1))

        def both(x, y):
            x = 0.5 * (cells + x)
            y = 0.5 * (cells + y)
            x = jnp.where(right_half, x[:, 128:], x[:, :128])
            y = jnp.where(right_half, y[:, 128:], y[:, :128])
            return jnp.where(
                odd,
                jnp.where(low, pltpu.roll(x, 64, 1), y),
                jnp.where(low, x, pltpu.roll(y, 64, 1)),
            )

        coef_ref[k, pl.ds(0, 8), :] = both(up, down)
        coef_ref[k, pl.ds(8, 8), :] = both(left, right)


def load_kernel(own_ref, got_ref, coef_ref, diff_ref, total_ref):
    _, place = here()
    lane, sub = lanes_of(), subs_of()
    low = lane < 64
    even = row_group(place) % 2 == 0
    over = (sub == 0) & jnp.logical_not(even)
    under = (sub == 7) & even
    inner_up = sub > 0
    inner_down = sub < 7

    def load(group, carry):
        tail = got_ref[group, pl.ds(ROWS - 8, 8), :]
        beside = jnp.where(
            sub < 6, pltpu.roll(tail, 7, 0), pltpu.roll(pltpu.roll(tail, 96, 1), 5, 0)
        )
        made = []
        for p in range(PAIRS):
            cells = got_ref[group, pl.ds(8 * p, 8), :]
            halo = got_ref[group, pl.ds(HALO + p, 1), :]
            above = jnp.where(over, halo, 0.0)
            below = jnp.where(under, halo, 0.0)
            up = cells - jnp.where(inner_up, pltpu.roll(cells, 1, 0), above)
            down = cells - jnp.where(inner_down, pltpu.roll(cells, 7, 0), below)
            left = cells - jnp.where(
                lane % 64 == 0, pltpu.roll(beside, (128 - 2 * p) % 128, 1), pltpu.roll(cells, 1, 1)
            )
            right = cells - jnp.where(
                lane % 64 == 63, pltpu.roll(beside, 62 - 2 * p, 1), pltpu.roll(cells, 127, 1)
            )
            vert = pltpu.roll(jnp.where(low, down, up), 64, 1)
            hori = pltpu.roll(jnp.where(low, right, left), 64, 1)
            made.append((p, jnp.where(low, up, vert), jnp.where(low, left, hori)))
            made.append((p + PAIRS, jnp.where(low, vert, down), jnp.where(low, hori, right)))
        coef_v = coef_ref[0, pl.ds(0, 8), :]
        coef_h = coef_ref[0, pl.ds(8, 8), :]
        for i, vert, hori in made:
            slot = group * (2 * PAIRS) + i
            diff_ref[slot, pl.ds(0, 8), :] = vert
            diff_ref[slot, pl.ds(8, 8), :] = hori
            total_ref[slot] = own_ref[pl.ds(slot, 1), :] * (coef_v * vert + coef_h * hori)
        return carry

    lax.fori_loop(0, got_ref.shape[0], load, 0, unroll=2)


def mix_kernel(
    place_ref, own_ref, weight_ref, diff_ref, start_ref, edge_ref, coef_ref, out_ref, diff, total, places, sem
):
    copy = pltpu.make_async_copy(place_ref, places, sem)
    copy.start()
    _, place = here()
    lane, sub = lanes_of(), subs_of()
    low = lane < 64
    groups = out_ref.shape[0]
    even = row_group(place) % 2 == 0
    meets = jnp.where(
        (low & (sub == 0) & even) | ((lane >= 64) & (sub == 7) & jnp.logical_not(even)), 1.0, 0.0
    )

    def patch(group, carry):
        edge = edge_ref[pl.ds(pl.multiple_of(8 * group, 8), 8), :]
        more = edge_ref[pl.ds(8 * groups + group, 1), :]
        rows = []
        for part in (edge, more):
            turned = pltpu.roll(part, 64, 1)
            rows.append((jnp.where(even, part, turned), jnp.where(even, turned, part)))
        coef_v = coef_ref[0, pl.ds(0, 8), :]
        made = []
        for p in range(PAIRS):
            for o in range(2):
                slot = group * (2 * PAIRS) + o * PAIRS + p
                beyond = meets * (rows[0][o][p : p + 1] if p < 8 else rows[1][o])
                vert = diff_ref[slot, pl.ds(0, 8), :] - beyond
                hori = diff_ref[slot, pl.ds(8, 8), :]
                made.append((slot, vert, hori, start_ref[slot] - own_ref[pl.ds(slot, 1), :] * (coef_v * beyond)))
        for slot, vert, hori, value in made:
            diff[slot, pl.ds(0, 8), :] = vert
            diff[slot, pl.ds(8, 8), :] = hori
            total[slot] = value
        return carry

    lax.fori_loop(0, groups, patch, 0, unroll=4)
    copy.wait()

    def couple(step, carry):
        terms = [6 * step + i for i in range(6)]
        uppers, gains, mine = [], [], []
        for term in terms:
            lower = places[term]
            vert = diff[lower, pl.ds(0, 8), :]
            hori = diff[lower, pl.ds(8, 8), :]
            parts = []
            for v in range(VARS):
                coef_v = coef_ref[v + 1, pl.ds(0, 8), :]
                coef_h = coef_ref[v + 1, pl.ds(8, 8), :]
                upper = places[LOWER + term * VARS + v]
                uppers.append(upper)
                parts.append(
                    weight_ref[term, pl.ds(v, 1), :]
                    * (coef_v * diff[upper, pl.ds(0, 8), :] + coef_h * diff[upper, pl.ds(8, 8), :])
                )
                gains.append(weight_ref[term, pl.ds(VARS + v, 1), :] * (coef_v * vert + coef_h * hori))
            while len(parts) > 1:
                parts = [x + y for x, y in zip(parts[::2], parts[1::2])] + parts[len(parts) // 2 * 2 :]
            mine.append(parts[0])
        for i, term in enumerate(terms):
            lower = places[term]
            total[lower] = total[lower] + mine[i]
            sums = [total[uppers[i * VARS + v]] + gains[i * VARS + v] for v in range(VARS)]
            for v in range(VARS):
                total[uppers[i * VARS + v]] = sums[v]
        return carry

    lax.fori_loop(0, LOWER // 6, couple, 0)

    def store(group, carry):
        made = []
        for p in range(PAIRS):
            a = total[group * (2 * PAIRS) + p]
            b = total[group * (2 * PAIRS) + PAIRS + p]
            made.append(jnp.where(low, a, b) + pltpu.roll(jnp.where(low, b, a), 64, 1))
        for p in range(PAIRS):
            out_ref[group, pl.ds(8 * p, 8), :] = made[p]
        return carry

    lax.fori_loop(0, groups, store, 0, unroll=8)


def unpack_kernel(got_ref, result_ref, out_ref, sem):
    low = lanes_of() < 64
    mask, _ = here()

    def send(r):
        rows = pl.ds(8 * r, 8)
        return pltpu.make_async_copy(out_ref.at[:, rows], result_ref.at[:, rows], sem.at[r])

    for r in range(4):
        for h in range(2):
            for p in range(PAIRS):
                one = got_ref[rank(holder(r, 2 * h) ^ mask), pl.ds(8 * p, 8), :]
                two = got_ref[rank(holder(r, 2 * h + 1) ^ mask), pl.ds(8 * p, 8), :]
                out_ref[p, pl.ds(8 * r, 8), pl.ds(128 * h, 128)] = jnp.where(
                    low, one, pltpu.roll(two, 64, 1)
                )
                out_ref[p + PAIRS, pl.ds(8 * r, 8), pl.ds(128 * h, 128)] = jnp.where(
                    low, pltpu.roll(one, 64, 1), two
                )
        send(r).start()
    for r in range(4):
        send(r).wait()


def vmem():
    return pl.BlockSpec(memory_space=pltpu.VMEM)


def hbm():
    return pl.BlockSpec(memory_space=pltpu.HBM)


def f32(*shape):
    return jax.ShapeDtypeStruct(shape, jnp.float32)


PARAMS = pltpu.CompilerParams(vmem_limit_bytes=32 * 1024 * 1024)


def cost(micros):
    return pl.CostEstimate(flops=0, bytes_accessed=micros * 3000000, transcendentals=0)


def pack(fields, groups):
    return pl.pallas_call(
        pack_kernel,
        out_shape=f32(groups, ROWS, 128),
        in_specs=[vmem()],
        out_specs=hbm(),
        scratch_shapes=[
            pltpu.VMEM((groups, ROWS, 128), jnp.float32),
            pltpu.SemaphoreType.DMA((groups,)),
        ],
        compiler_params=PARAMS,
        cost_estimate=cost(2),
    )(fields)


def edges(got):
    return pl.pallas_call(
        edge_kernel,
        out_shape=f32(got.shape[0] * PAIRS, 128),
        in_specs=[vmem()],
        out_specs=vmem(),
        compiler_params=PARAMS,
        cost_estimate=cost(1),
    )(got)


def coefs(modes, edge, weights):
    return pl.pallas_call(
        coef_kernel,
        out_shape=f32(modes.shape[0], 16, 128),
        in_specs=[vmem(), vmem(), hbm()],
        out_specs=vmem(),
        compiler_params=PARAMS,
        cost_estimate=cost(1),
    )(modes, edge, weights)


def load(own, got, coef):
    slots = got.shape[0] * 2 * PAIRS
    return pl.pallas_call(
        load_kernel,
        out_shape=(f32(slots, 16, 128), f32(slots, 8, 128)),
        in_specs=[vmem()] * 3,
        out_specs=(vmem(), vmem()),
        compiler_params=PARAMS,
        cost_estimate=cost(4),
    )(own, got, coef)


def mix(places, own, weights, diff, total, edge, coef):
    slots = diff.shape[0]
    return pl.pallas_call(
        mix_kernel,
        out_shape=f32(slots // (2 * PAIRS), BLOCK, 128),
        in_specs=[vmem()] * 7,
        out_specs=vmem(),
        scratch_shapes=[
            pltpu.VMEM((slots, 16, 128), jnp.float32),
            pltpu.VMEM((slots, 8, 128), jnp.float32),
            pltpu.SMEM(places.shape, jnp.int32),
            pltpu.SemaphoreType.DMA,
        ],
        compiler_params=PARAMS,
        cost_estimate=cost(5),
    )(places, own, weights, diff, total, edge, coef)


def unpack(got, shape):
    return pl.pallas_call(
        unpack_kernel,
        out_shape=f32(*shape),
        in_specs=[vmem()],
        out_specs=hbm(),
        scratch_shapes=[pltpu.VMEM(shape, jnp.float32), pltpu.SemaphoreType.DMA((4,))],
        compiler_params=PARAMS,
        cost_estimate=cost(1),
    )(got)


def tables(pair_list, pair_value, assign):
    terms = assign.shape[0]
    numbers = jnp.arange(terms, dtype=jnp.int32)
    row, col, mode = pair_list[:, 0:1], pair_list[:, 1:2], pair_list[:, 2:3]
    slot = jnp.sum(jnp.where(col == assign[None, :], numbers[None, :], 0), axis=1, keepdims=True)
    at = jnp.minimum(row, col) == numbers[None, :]
    kinds = jnp.arange(1 + 3 * VARS, dtype=jnp.int32)[None, :]
    wanted = jnp.where(kinds <= VARS, kinds, (kinds - 1) % VARS + 1)
    side = jnp.where(kinds <= VARS, row <= col, jnp.where(kinds <= 2 * VARS, row > col, row < col))
    value = jnp.where(kinds <= 2 * VARS, pair_value[:, None], slot.astype(jnp.float32))
    value = jnp.where((mode == wanted) & side, value, 0.0)
    found = lax.dot_general(
        at.astype(jnp.float32),
        value,
        (((0,), (0,)), ((), ())),
        precision=lax.Precision.HIGHEST,
        preferred_element_type=jnp.float32,
    )
    coupled = jnp.pad(found[:LOWER, 1 : 1 + 2 * VARS], ((0, 0), (0, 4)))
    uppers = jnp.round(found[:LOWER, 1 + 2 * VARS :]).astype(jnp.int32).reshape(-1)
    weights = jnp.broadcast_to(coupled[:, :, None], coupled.shape + (128,))
    held = assign[:, None] == numbers[None, :]
    own = jnp.sum(jnp.where(held, found[:, 0][None, :], 0.0), axis=1, keepdims=True)
    lowers = jnp.sum(jnp.where(held[:, :LOWER], numbers[:, None], 0), axis=0)
    places = jnp.pad(jnp.concatenate([lowers, uppers]), (0, 1024 - LOWER * (1 + VARS)))
    return places, jnp.broadcast_to(own, (terms, 128)), weights


def shards(fields, modes, pair_list, pair_value, assign):
    groups = lax.axis_size("term")
    count = lax.axis_size("space")
    passes, between = [], []
    for c in range(groups // 4):
        for s in range(count):
            one, two = ((holder(r, c) ^ mask_at(s)) * count + s for r in (1, 2))
            between += [(one, two), (two, one)]
        for s in range(count - 1):
            lower = (holder(0, c) ^ mask_at(s + 1)) * count + s + 1
            upper = (holder(3, c) ^ mask_at(s)) * count + s
            passes += [(lower, upper), (upper, lower)]
    order = sorted(range(groups), key=rank)
    assign = assign.reshape(groups, -1)[jnp.array(order)].reshape(-1)
    sent = pack(fields, groups)
    sent, modes = lax.optimization_barrier((sent, modes))
    got = lax.all_to_all(sent, "term", 0, 0, axis_index_groups=[order], tiled=True)
    places, own, weights = tables(pair_list, pair_value, assign)
    _, place = here()
    edge = jnp.where(row_group(place) == 0, modes[:, 0], modes[:, modes.shape[1] - 1])
    coef = coefs(modes, lax.ppermute(edge, ("term", "space"), passes), weights)
    got, coef, places, own = lax.optimization_barrier((got, coef, places, own))
    beyond = lax.ppermute(edges(got), ("term", "space"), passes + between)
    diff, total = load(own, got, coef)
    mixed = mix(places, own, weights, diff, total, beyond, coef)
    back = lax.all_to_all(mixed, "term", 0, 0, axis_index_groups=[order], tiled=True)
    return unpack(back, fields.shape)


def solution(mesh):
    return jax.shard_map(
        shards,
        mesh=mesh,
        in_specs=(P("term", "space", None), P(None, "space", None), P(), P(), P()),
        out_specs=P("term", "space", None),
        check_vma=False,
    )
```

```python
import jax
import jax.numpy as jnp
from jax import lax
from jax.experimental import pallas as pl
from jax.experimental.pallas import tpu as pltpu
from jax.sharding import PartitionSpec as P

PAIRS = 9
BLOCK = 8 * PAIRS
ROWS = 88
HALO = 72
SIDE = 81
LOWER = 66
VARS = 10


def holder(r, c):
    return 4 * c + (r ^ c)


def rank(device):
    device = device ^ 15
    return (device & 1) << 3 | (device & 2) << 1 | (device & 4) >> 1 | (device >> 3 ^ 1)


def mask_at(space):
    return (space >> 1 & 1) * 8 + (space & 1) * 3


def here():
    mask = mask_at(lax.axis_index("space"))
    return mask, lax.axis_index("term") ^ mask


def row_group(place):
    return (place & 3) ^ (place >> 2)


def lanes_of(shape=(8, 128)):
    return lax.broadcasted_iota(jnp.int32, shape, 1)


def subs_of(shape=(8, 128)):
    return lax.broadcasted_iota(jnp.int32, shape, 0)


def pack_kernel(f_ref, sent_ref, out_ref, out_sem):
    lane = lanes_of()
    low = lane < 64
    even = lane % 2 == 0
    spare = lane % 64 >= 32
    mask, _ = here()

    def send(r, c):
        to = rank(holder(r, c) ^ mask)
        return pltpu.make_async_copy(out_ref.at[to], sent_ref.at[to], out_sem.at[4 * r + c])

    for r in range(4):
        near, far = [], []
        for h in range(2):
            ga = jnp.zeros((8, 128), jnp.float32)
            gb = jnp.zeros((8, 128), jnp.float32)
            for p in range(PAIRS):
                a = f_ref[p, pl.ds(8 * r, 8), pl.ds(128 * h, 128)]
                b = f_ref[p + PAIRS, pl.ds(8 * r, 8), pl.ds(128 * h, 128)]
                both = (
                    jnp.where(low, a, pltpu.roll(b, 64, 1)),
                    jnp.where(low, pltpu.roll(a, 64, 1), b),
                )
                for o in range(2):
                    c = 2 * h + o
                    first, last = both[o][0:1], both[o][7:8]
                    out_ref[rank(holder(r, c) ^ mask), pl.ds(8 * p, 8), :] = both[o]
                    if r % 2 == 0:
                        out_ref[rank(holder(r + 1, c) ^ mask), pl.ds(HALO + p, 1), :] = last
                    else:
                        out_ref[rank(holder(r - 1, c) ^ mask), pl.ds(HALO + p, 1), :] = first
                pair = (lane % 64) // 2 == p
                ga = jnp.where(pair, pltpu.roll(a, (2 * p - 63) % 128, 1), ga)
                gb = jnp.where(pair, pltpu.roll(b, 2 * p + 1, 1), gb)
            near.append(jnp.where(low, ga, gb))
            far.append(pltpu.roll(jnp.where(low, gb, ga), 64, 1))
        zero = jnp.zeros((8, 128), jnp.float32)
        sides = (
            jnp.where(even, zero, near[0]),
            jnp.where(even, near[0], far[1]),
            jnp.where(even, far[0], near[1]),
            jnp.where(even, near[1], zero),
        )
        for c in range(4):
            moved = pltpu.roll(pltpu.roll(sides[c], 32, 1), 2, 0)
            kept = jnp.where(spare, moved, sides[c])
            out_ref[rank(holder(r, c) ^ mask), pl.ds(SIDE, 7), :] = kept[0:7]
        for done in (r - 1, r):
            if r % 2 == 1:
                for c in range(4):
                    send(done, c).start()
    for r in range(4):
        for c in range(4):
            send(r, c).wait()


def edge_kernel(got_ref, edge_ref):
    _, place = here()
    groups = got_ref.shape[0]
    even = row_group(place) % 2 == 0
    for row, wanted in ((0, even), (7, jnp.logical_not(even))):

        @pl.when(wanted)
        def _():
            for group in range(groups):
                edge_ref[pl.ds(8 * group, 8), :] = got_ref[group, pl.ds(row, 8, stride=8), :]
                edge_ref[pl.ds(8 * groups + group, 1), :] = got_ref[group, pl.ds(64 + row, 1), :]


def coef_kernel(modes_ref, edge_ref, weight_ref, coef_ref):
    _, place = here()
    low = lanes_of() < 64
    block_row = row_group(place)
    block_col = place >> 2
    first = block_row == 0
    last = block_row == 3
    odd = block_col % 2 == 1
    right_half = block_col >= 2
    lane = lanes_of((8, 256))
    sub = subs_of((8, 256))
    for k in range(modes_ref.shape[0]):
        cells = modes_ref[k, pl.ds(pl.multiple_of(8 * block_row, 8), 8), :]
        before = modes_ref[k, pl.ds(pl.multiple_of(8 * jnp.maximum(block_row - 1, 0), 8), 8), :]
        after = modes_ref[k, pl.ds(pl.multiple_of(8 * jnp.minimum(block_row + 1, 3), 8), 8), :]
        over = jnp.where(first, edge_ref[pl.ds(k, 1), :], before[7:8])
        under = jnp.where(last, edge_ref[pl.ds(k, 1), :], after[0:1])
        up = jnp.where(sub == 0, over, pltpu.roll(cells, 1, 0))
        down = jnp.where(sub == 7, under, pltpu.roll(cells, 7, 0))
        left = jnp.where(lane == 0, 0.0, pltpu.roll(cells, 1, 1))
        right = jnp.where(lane == 255, 0.0, pltpu.roll(cells, 255, 1))

        def both(x, y):
            x = 0.5 * (cells + x)
            y = 0.5 * (cells + y)
            x = jnp.where(right_half, x[:, 128:], x[:, :128])
            y = jnp.where(right_half, y[:, 128:], y[:, :128])
            return jnp.where(
                odd,
                jnp.where(low, pltpu.roll(x, 64, 1), y),
                jnp.where(low, x, pltpu.roll(y, 64, 1)),
            )

        coef_ref[k, pl.ds(0, 8), :] = both(up, down)
        coef_ref[k, pl.ds(8, 8), :] = both(left, right)


def load_kernel(own_ref, got_ref, coef_ref, diff_ref, total_ref):
    _, place = here()
    lane, sub = lanes_of(), subs_of()
    low = lane < 64
    even = row_group(place) % 2 == 0
    over = (sub == 0) & jnp.logical_not(even)
    under = (sub == 7) & even
    inner_up = sub > 0
    inner_down = sub < 7

    def load(group, carry):
        tail = got_ref[group, pl.ds(ROWS - 8, 8), :]
        beside = jnp.where(
            sub < 6, pltpu.roll(tail, 7, 0), pltpu.roll(pltpu.roll(tail, 96, 1), 5, 0)
        )
        made = []
        for p in range(PAIRS):
            cells = got_ref[group, pl.ds(8 * p, 8), :]
            halo = got_ref[group, pl.ds(HALO + p, 1), :]
            above = jnp.where(over, halo, 0.0)
            below = jnp.where(under, halo, 0.0)
            up = cells - jnp.where(inner_up, pltpu.roll(cells, 1, 0), above)
            down = cells - jnp.where(inner_down, pltpu.roll(cells, 7, 0), below)
            left = cells - jnp.where(
                lane % 64 == 0, pltpu.roll(beside, (128 - 2 * p) % 128, 1), pltpu.roll(cells, 1, 1)
            )
            right = cells - jnp.where(
                lane % 64 == 63, pltpu.roll(beside, 62 - 2 * p, 1), pltpu.roll(cells, 127, 1)
            )
            vert = pltpu.roll(jnp.where(low, down, up), 64, 1)
            hori = pltpu.roll(jnp.where(low, right, left), 64, 1)
            made.append((p, jnp.where(low, up, vert), jnp.where(low, left, hori)))
            made.append((p + PAIRS, jnp.where(low, vert, down), jnp.where(low, hori, right)))
        coef_v = coef_ref[0, pl.ds(0, 8), :]
        coef_h = coef_ref[0, pl.ds(8, 8), :]
        for i, vert, hori in made:
            slot = group * (2 * PAIRS) + i
            diff_ref[slot, pl.ds(0, 8), :] = vert
            diff_ref[slot, pl.ds(8, 8), :] = hori
            total_ref[slot] = own_ref[pl.ds(slot, 1), :] * (coef_v * vert + coef_h * hori)
        return carry

    lax.fori_loop(0, got_ref.shape[0], load, 0, unroll=2)


def mix_kernel(
    place_ref, own_ref, weight_ref, diff_ref, start_ref, edge_ref, coef_ref, out_ref, diff, total, places, sem
):
    copy = pltpu.make_async_copy(place_ref, places, sem)
    copy.start()
    _, place = here()
    lane, sub = lanes_of(), subs_of()
    low = lane < 64
    groups = out_ref.shape[0]
    even = row_group(place) % 2 == 0
    meets = jnp.where(
        (low & (sub == 0) & even) | ((lane >= 64) & (sub == 7) & jnp.logical_not(even)), 1.0, 0.0
    )

    def patch(group, carry):
        edge = edge_ref[pl.ds(pl.multiple_of(8 * group, 8), 8), :]
        more = edge_ref[pl.ds(8 * groups + group, 1), :]
        rows = []
        for part in (edge, more):
            turned = pltpu.roll(part, 64, 1)
            rows.append((jnp.where(even, part, turned), jnp.where(even, turned, part)))
        coef_v = coef_ref[0, pl.ds(0, 8), :]
        made = []
        for p in range(PAIRS):
            for o in range(2):
                slot = group * (2 * PAIRS) + o * PAIRS + p
                beyond = meets * (rows[0][o][p : p + 1] if p < 8 else rows[1][o])
                vert = diff_ref[slot, pl.ds(0, 8), :] - beyond
                hori = diff_ref[slot, pl.ds(8, 8), :]
                made.append((slot, vert, hori, start_ref[slot] - own_ref[pl.ds(slot, 1), :] * (coef_v * beyond)))
        for slot, vert, hori, value in made:
            diff[slot, pl.ds(0, 8), :] = vert
            diff[slot, pl.ds(8, 8), :] = hori
            total[slot, pl.ds(0, 8), :] = value
        return carry

    lax.fori_loop(0, groups, patch, 0, unroll=4)
    copy.wait()

    def couple(step, carry):
        terms = [6 * step + i for i in range(6)]
        uppers, gains, mine = [], [], []
        for term in terms:
            lower = places[term]
            vert = diff[lower, pl.ds(0, 8), :]
            hori = diff[lower, pl.ds(8, 8), :]
            parts = []
            for v in range(VARS):
                coef_v = coef_ref[v + 1, pl.ds(0, 8), :]
                coef_h = coef_ref[v + 1, pl.ds(8, 8), :]
                upper = places[LOWER + term * VARS + v]
                uppers.append(upper)
                parts.append(
                    weight_ref[term, pl.ds(v, 1), :]
                    * (coef_v * diff[upper, pl.ds(0, 8), :] + coef_h * diff[upper, pl.ds(8, 8), :])
                )
                gains.append(weight_ref[term, pl.ds(VARS + v, 1), :] * (coef_v * vert + coef_h * hori))
            while len(parts) > 1:
                parts = [x + y for x, y in zip(parts[::2], parts[1::2])] + parts[len(parts) // 2 * 2 :]
            mine.append(parts[0])
        for i, term in enumerate(terms):
            lower = places[term]
            total[lower, pl.ds(0, 8), :] = total[lower, pl.ds(0, 8), :] + mine[i]
            sums = [total[uppers[i * VARS + v], pl.ds(0, 8), :] + gains[i * VARS + v] for v in range(VARS)]
            for v in range(VARS):
                total[uppers[i * VARS + v], pl.ds(0, 8), :] = sums[v]
        return carry

    lax.fori_loop(0, LOWER // 6, couple, 0, unroll=2)

    def store(group, carry):
        made = []
        for p in range(PAIRS):
            a = total[group * (2 * PAIRS) + p, pl.ds(0, 8), :]
            b = total[group * (2 * PAIRS) + PAIRS + p, pl.ds(0, 8), :]
            made.append(jnp.where(low, a, b) + pltpu.roll(jnp.where(low, b, a), 64, 1))
        for p in range(PAIRS):
            out_ref[group, pl.ds(8 * p, 8), :] = made[p]
        return carry

    lax.fori_loop(0, groups, store, 0, unroll=16)


def unpack_kernel(got_ref, result_ref, out_ref, sem):
    low = lanes_of() < 64
    mask, _ = here()

    def send(r):
        rows = pl.ds(8 * r, 8)
        return pltpu.make_async_copy(out_ref.at[:, rows], result_ref.at[:, rows], sem.at[r])

    for r in range(4):
        for h in range(2):
            for p in range(PAIRS):
                one = got_ref[rank(holder(r, 2 * h) ^ mask), pl.ds(8 * p, 8), :]
                two = got_ref[rank(holder(r, 2 * h + 1) ^ mask), pl.ds(8 * p, 8), :]
                out_ref[p, pl.ds(8 * r, 8), pl.ds(128 * h, 128)] = jnp.where(
                    low, one, pltpu.roll(two, 64, 1)
                )
                out_ref[p + PAIRS, pl.ds(8 * r, 8), pl.ds(128 * h, 128)] = jnp.where(
                    low, pltpu.roll(one, 64, 1), two
                )
        send(r).start()
    for r in range(4):
        send(r).wait()


def vmem():
    return pl.BlockSpec(memory_space=pltpu.VMEM)


def hbm():
    return pl.BlockSpec(memory_space=pltpu.HBM)


def f32(*shape):
    return jax.ShapeDtypeStruct(shape, jnp.float32)


PARAMS = pltpu.CompilerParams(vmem_limit_bytes=32 * 1024 * 1024)


def cost(micros):
    return pl.CostEstimate(flops=0, bytes_accessed=micros * 3000000, transcendentals=0)


def pack(fields, groups):
    return pl.pallas_call(
        pack_kernel,
        out_shape=f32(groups, ROWS, 128),
        in_specs=[vmem()],
        out_specs=hbm(),
        scratch_shapes=[
            pltpu.VMEM((groups, ROWS, 128), jnp.float32),
            pltpu.SemaphoreType.DMA((groups,)),
        ],
        compiler_params=PARAMS,
        cost_estimate=cost(2),
    )(fields)


def edges(got):
    return pl.pallas_call(
        edge_kernel,
        out_shape=f32(got.shape[0] * PAIRS, 128),
        in_specs=[vmem()],
        out_specs=vmem(),
        compiler_params=PARAMS,
        cost_estimate=cost(1),
    )(got)


def coefs(modes, edge, weights):
    return pl.pallas_call(
        coef_kernel,
        out_shape=f32(modes.shape[0], 16, 128),
        in_specs=[vmem(), vmem(), hbm()],
        out_specs=vmem(),
        compiler_params=PARAMS,
        cost_estimate=cost(1),
    )(modes, edge, weights)


def load(own, got, coef):
    slots = got.shape[0] * 2 * PAIRS
    return pl.pallas_call(
        load_kernel,
        out_shape=(f32(slots, 16, 128), f32(slots, 8, 128)),
        in_specs=[vmem()] * 3,
        out_specs=(vmem(), vmem()),
        compiler_params=PARAMS,
        cost_estimate=cost(4),
    )(own, got, coef)


def mix(places, own, weights, diff, total, edge, coef):
    slots = diff.shape[0]
    return pl.pallas_call(
        mix_kernel,
        out_shape=f32(slots // (2 * PAIRS), BLOCK, 128),
        in_specs=[vmem()] * 7,
        out_specs=vmem(),
        scratch_shapes=[
            pltpu.VMEM((slots, 16, 128), jnp.float32),
            pltpu.VMEM((slots, 16, 128), jnp.float32),
            pltpu.SMEM(places.shape, jnp.int32),
            pltpu.SemaphoreType.DMA,
        ],
        compiler_params=PARAMS,
        cost_estimate=cost(5),
    )(places, own, weights, diff, total, edge, coef)


def unpack(got, shape):
    return pl.pallas_call(
        unpack_kernel,
        out_shape=f32(*shape),
        in_specs=[vmem()],
        out_specs=hbm(),
        scratch_shapes=[pltpu.VMEM(shape, jnp.float32), pltpu.SemaphoreType.DMA((4,))],
        compiler_params=PARAMS,
        cost_estimate=cost(1),
    )(got)


def tables(pair_list, pair_value, assign):
    terms = assign.shape[0]
    numbers = jnp.arange(terms, dtype=jnp.int32)
    row, col, mode = pair_list[:, 0:1], pair_list[:, 1:2], pair_list[:, 2:3]
    slot = jnp.sum(jnp.where(col == assign[None, :], numbers[None, :], 0), axis=1, keepdims=True)
    at = jnp.minimum(row, col) == numbers[None, :]
    kinds = jnp.arange(1 + 3 * VARS, dtype=jnp.int32)[None, :]
    wanted = jnp.where(kinds <= VARS, kinds, (kinds - 1) % VARS + 1)
    side = jnp.where(kinds <= VARS, row <= col, jnp.where(kinds <= 2 * VARS, row > col, row < col))
    value = jnp.where(kinds <= 2 * VARS, pair_value[:, None], slot.astype(jnp.float32))
    value = jnp.where((mode == wanted) & side, value, 0.0)
    found = lax.dot_general(
        at.astype(jnp.float32),
        value,
        (((0,), (0,)), ((), ())),
        precision=lax.Precision.HIGHEST,
        preferred_element_type=jnp.float32,
    )
    coupled = jnp.pad(found[:LOWER, 1 : 1 + 2 * VARS], ((0, 0), (0, 4)))
    uppers = jnp.round(found[:LOWER, 1 + 2 * VARS :]).astype(jnp.int32).reshape(-1)
    weights = jnp.broadcast_to(coupled[:, :, None], coupled.shape + (128,))
    held = assign[:, None] == numbers[None, :]
    own = jnp.sum(jnp.where(held, found[:, 0][None, :], 0.0), axis=1, keepdims=True)
    lowers = jnp.sum(jnp.where(held[:, :LOWER], numbers[:, None], 0), axis=0)
    places = jnp.pad(jnp.concatenate([lowers, uppers]), (0, 1024 - LOWER * (1 + VARS)))
    return places, jnp.broadcast_to(own, (terms, 128)), weights


def shards(fields, modes, pair_list, pair_value, assign):
    groups = lax.axis_size("term")
    count = lax.axis_size("space")
    passes, between = [], []
    for c in range(groups // 4):
        for s in range(count):
            one, two = ((holder(r, c) ^ mask_at(s)) * count + s for r in (1, 2))
            between += [(one, two), (two, one)]
        for s in range(count - 1):
            lower = (holder(0, c) ^ mask_at(s + 1)) * count + s + 1
            upper = (holder(3, c) ^ mask_at(s)) * count + s
            passes += [(lower, upper), (upper, lower)]
    order = sorted(range(groups), key=rank)
    assign = assign.reshape(groups, -1)[jnp.array(order)].reshape(-1)
    sent = pack(fields, groups)
    sent, modes = lax.optimization_barrier((sent, modes))
    got = lax.all_to_all(sent, "term", 0, 0, axis_index_groups=[order], tiled=True)
    places, own, weights = tables(pair_list, pair_value, assign)
    _, place = here()
    edge = jnp.where(row_group(place) == 0, modes[:, 0], modes[:, modes.shape[1] - 1])
    coef = coefs(modes, lax.ppermute(edge, ("term", "space"), passes), weights)
    got, coef, places, own = lax.optimization_barrier((got, coef, places, own))
    beyond = lax.ppermute(edges(got), ("term", "space"), passes + between)
    diff, total = load(own, got, coef)
    mixed = mix(places, own, weights, diff, total, beyond, coef)
    back = lax.all_to_all(mixed, "term", 0, 0, axis_index_groups=[order], tiled=True)
    return unpack(back, fields.shape)


def solution(mesh):
    return jax.shard_map(
        shards,
        mesh=mesh,
        in_specs=(P("term", "space", None), P(None, "space", None), P(), P(), P()),
        out_specs=P("term", "space", None),
        check_vma=False,
    )
```

```python
import jax
import jax.numpy as jnp
from jax import lax
from jax.experimental import pallas as pl
from jax.experimental.pallas import tpu as pltpu
from jax.sharding import PartitionSpec as P

PAIRS = 9
BLOCK = 8 * PAIRS
ROWS = 88
HALO = 72
SIDE = 81
LOWER = 66
VARS = 10


def holder(r, c):
    return 4 * c + (r ^ c)


def rank(device):
    device = device ^ 15
    return (device & 1) << 3 | (device & 2) << 1 | (device & 4) >> 1 | (device >> 3 ^ 1)


def mask_at(space):
    return (space >> 1 & 1) * 8 + (space & 1) * 3


def here():
    mask = mask_at(lax.axis_index("space"))
    return mask, lax.axis_index("term") ^ mask


def row_group(place):
    return (place & 3) ^ (place >> 2)


def lanes_of(shape=(8, 128)):
    return lax.broadcasted_iota(jnp.int32, shape, 1)


def subs_of(shape=(8, 128)):
    return lax.broadcasted_iota(jnp.int32, shape, 0)


def pack_kernel(f_ref, sent_ref, out_ref, out_sem):
    lane = lanes_of()
    low = lane < 64
    even = lane % 2 == 0
    spare = lane % 64 >= 32
    mask, _ = here()

    def send(r, c, part):
        to = rank(holder(r, c) ^ mask)
        rows = pl.ds(0, BLOCK) if part == 0 else pl.ds(BLOCK, ROWS - BLOCK)
        return pltpu.make_async_copy(
            out_ref.at[to, rows], sent_ref.at[to, rows], out_sem.at[part, 4 * r + c]
        )

    for r in range(4):
        near, far = [], []
        for h in range(2):
            ga = jnp.zeros((8, 128), jnp.float32)
            gb = jnp.zeros((8, 128), jnp.float32)
            for p in range(PAIRS):
                a = f_ref[p, pl.ds(8 * r, 8), pl.ds(128 * h, 128)]
                b = f_ref[p + PAIRS, pl.ds(8 * r, 8), pl.ds(128 * h, 128)]
                both = (
                    jnp.where(low, a, pltpu.roll(b, 64, 1)),
                    jnp.where(low, pltpu.roll(a, 64, 1), b),
                )
                for o in range(2):
                    c = 2 * h + o
                    first, last = both[o][0:1], both[o][7:8]
                    out_ref[rank(holder(r, c) ^ mask), pl.ds(8 * p, 8), :] = both[o]
                    if r % 2 == 0:
                        out_ref[rank(holder(r + 1, c) ^ mask), pl.ds(HALO + p, 1), :] = last
                    else:
                        out_ref[rank(holder(r - 1, c) ^ mask), pl.ds(HALO + p, 1), :] = first
                pair = (lane % 64) // 2 == p
                ga = jnp.where(pair, pltpu.roll(a, (2 * p - 63) % 128, 1), ga)
                gb = jnp.where(pair, pltpu.roll(b, 2 * p + 1, 1), gb)
            near.append(jnp.where(low, ga, gb))
            far.append(pltpu.roll(jnp.where(low, gb, ga), 64, 1))
        zero = jnp.zeros((8, 128), jnp.float32)
        sides = (
            jnp.where(even, zero, near[0]),
            jnp.where(even, near[0], far[1]),
            jnp.where(even, far[0], near[1]),
            jnp.where(even, near[1], zero),
        )
        for c in range(4):
            moved = pltpu.roll(pltpu.roll(sides[c], 32, 1), 2, 0)
            kept = jnp.where(spare, moved, sides[c])
            out_ref[rank(holder(r, c) ^ mask), pl.ds(SIDE, 7), :] = kept[0:7]
        for c in range(4):
            send(r, c, 0).start()
            if r % 2 == 1:
                send(r - 1, c, 1).start()
                send(r, c, 1).start()
    for r in range(4):
        for c in range(4):
            send(r, c, 0).wait()
            send(r, c, 1).wait()


def edge_kernel(got_ref, edge_ref):
    _, place = here()
    groups = got_ref.shape[0]
    even = row_group(place) % 2 == 0
    for row, wanted in ((0, even), (7, jnp.logical_not(even))):

        @pl.when(wanted)
        def _():
            for group in range(groups):
                edge_ref[pl.ds(8 * group, 8), :] = got_ref[group, pl.ds(row, 8, stride=8), :]
                edge_ref[pl.ds(8 * groups + group, 1), :] = got_ref[group, pl.ds(64 + row, 1), :]


def coef_kernel(modes_ref, edge_ref, weight_ref, coef_ref):
    _, place = here()
    low = lanes_of() < 64
    block_row = row_group(place)
    block_col = place >> 2
    first = block_row == 0
    last = block_row == 3
    odd = block_col % 2 == 1
    right_half = block_col >= 2
    lane = lanes_of((8, 256))
    sub = subs_of((8, 256))
    for k in range(modes_ref.shape[0]):
        cells = modes_ref[k, pl.ds(pl.multiple_of(8 * block_row, 8), 8), :]
        before = modes_ref[k, pl.ds(pl.multiple_of(8 * jnp.maximum(block_row - 1, 0), 8), 8), :]
        after = modes_ref[k, pl.ds(pl.multiple_of(8 * jnp.minimum(block_row + 1, 3), 8), 8), :]
        over = jnp.where(first, edge_ref[pl.ds(k, 1), :], before[7:8])
        under = jnp.where(last, edge_ref[pl.ds(k, 1), :], after[0:1])
        up = jnp.where(sub == 0, over, pltpu.roll(cells, 1, 0))
        down = jnp.where(sub == 7, under, pltpu.roll(cells, 7, 0))
        left = jnp.where(lane == 0, 0.0, pltpu.roll(cells, 1, 1))
        right = jnp.where(lane == 255, 0.0, pltpu.roll(cells, 255, 1))

        def both(x, y):
            x = 0.5 * (cells + x)
            y = 0.5 * (cells + y)
            x = jnp.where(right_half, x[:, 128:], x[:, :128])
            y = jnp.where(right_half, y[:, 128:], y[:, :128])
            return jnp.where(
                odd,
                jnp.where(low, pltpu.roll(x, 64, 1), y),
                jnp.where(low, x, pltpu.roll(y, 64, 1)),
            )

        coef_ref[k, pl.ds(0, 8), :] = both(up, down)
        coef_ref[k, pl.ds(8, 8), :] = both(left, right)


def load_kernel(own_ref, got_ref, coef_ref, diff_ref, total_ref):
    _, place = here()
    lane, sub = lanes_of(), subs_of()
    low = lane < 64
    even = row_group(place) % 2 == 0
    over = (sub == 0) & jnp.logical_not(even)
    under = (sub == 7) & even
    inner_up = sub > 0
    inner_down = sub < 7

    def load(group, carry):
        tail = got_ref[group, pl.ds(ROWS - 8, 8), :]
        beside = jnp.where(
            sub < 6, pltpu.roll(tail, 7, 0), pltpu.roll(pltpu.roll(tail, 96, 1), 5, 0)
        )
        made = []
        for p in range(PAIRS):
            cells = got_ref[group, pl.ds(8 * p, 8), :]
            halo = got_ref[group, pl.ds(HALO + p, 1), :]
            above = jnp.where(over, halo, 0.0)
            below = jnp.where(under, halo, 0.0)
            up = cells - jnp.where(inner_up, pltpu.roll(cells, 1, 0), above)
            down = cells - jnp.where(inner_down, pltpu.roll(cells, 7, 0), below)
            left = cells - jnp.where(
                lane % 64 == 0, pltpu.roll(beside, (128 - 2 * p) % 128, 1), pltpu.roll(cells, 1, 1)
            )
            right = cells - jnp.where(
                lane % 64 == 63, pltpu.roll(beside, 62 - 2 * p, 1), pltpu.roll(cells, 127, 1)
            )
            vert = pltpu.roll(jnp.where(low, down, up), 64, 1)
            hori = pltpu.roll(jnp.where(low, right, left), 64, 1)
            made.append((p, jnp.where(low, up, vert), jnp.where(low, left, hori)))
            made.append((p + PAIRS, jnp.where(low, vert, down), jnp.where(low, hori, right)))
        coef_v = coef_ref[0, pl.ds(0, 8), :]
        coef_h = coef_ref[0, pl.ds(8, 8), :]
        for i, vert, hori in made:
            slot = group * (2 * PAIRS) + i
            diff_ref[slot, pl.ds(0, 8), :] = vert
            diff_ref[slot, pl.ds(8, 8), :] = hori
            total_ref[slot] = own_ref[pl.ds(slot, 1), :] * (coef_v * vert + coef_h * hori)
        return carry

    lax.fori_loop(0, got_ref.shape[0], load, 0, unroll=2)


def mix_kernel(
    place_ref, own_ref, weight_ref, diff_ref, start_ref, edge_ref, coef_ref, out_ref, diff, total, places, sem
):
    copy = pltpu.make_async_copy(place_ref, places, sem)
    copy.start()
    _, place = here()
    lane, sub = lanes_of(), subs_of()
    low = lane < 64
    groups = out_ref.shape[0]
    even = row_group(place) % 2 == 0
    meets = jnp.where(
        (low & (sub == 0) & even) | ((lane >= 64) & (sub == 7) & jnp.logical_not(even)), 1.0, 0.0
    )

    def patch(group, carry):
        edge = edge_ref[pl.ds(pl.multiple_of(8 * group, 8), 8), :]
        more = edge_ref[pl.ds(8 * groups + group, 1), :]
        rows = []
        for part in (edge, more):
            turned = pltpu.roll(part, 64, 1)
            rows.append((jnp.where(even, part, turned), jnp.where(even, turned, part)))
        coef_v = coef_ref[0, pl.ds(0, 8), :]
        made = []
        for p in range(PAIRS):
            for o in range(2):
                slot = group * (2 * PAIRS) + o * PAIRS + p
                beyond = meets * (rows[0][o][p : p + 1] if p < 8 else rows[1][o])
                vert = diff_ref[slot, pl.ds(0, 8), :] - beyond
                hori = diff_ref[slot, pl.ds(8, 8), :]
                made.append((slot, vert, hori, start_ref[slot] - own_ref[pl.ds(slot, 1), :] * (coef_v * beyond)))
        for slot, vert, hori, value in made:
            diff[slot, pl.ds(0, 8), :] = vert
            diff[slot, pl.ds(8, 8), :] = hori
            total[slot, pl.ds(0, 8), :] = value
        return carry

    lax.fori_loop(0, groups, patch, 0, unroll=4)
    copy.wait()

    def couple(step, carry):
        terms = [6 * step + i for i in range(6)]
        uppers, gains, mine = [], [], []
        for term in terms:
            lower = places[term]
            vert = diff[lower, pl.ds(0, 8), :]
            hori = diff[lower, pl.ds(8, 8), :]
            parts = []
            for v in range(VARS):
                coef_v = coef_ref[v + 1, pl.ds(0, 8), :]
                coef_h = coef_ref[v + 1, pl.ds(8, 8), :]
                upper = places[LOWER + term * VARS + v]
                uppers.append(upper)
                parts.append(
                    weight_ref[term, pl.ds(v, 1), :]
                    * (coef_v * diff[upper, pl.ds(0, 8), :] + coef_h * diff[upper, pl.ds(8, 8), :])
                )
                gains.append(weight_ref[term, pl.ds(VARS + v, 1), :] * (coef_v * vert + coef_h * hori))
            while len(parts) > 1:
                parts = [x + y for x, y in zip(parts[::2], parts[1::2])] + parts[len(parts) // 2 * 2 :]
            mine.append(parts[0])
        for i, term in enumerate(terms):
            lower = places[term]
            total[lower, pl.ds(0, 8), :] = total[lower, pl.ds(0, 8), :] + mine[i]
            sums = [total[uppers[i * VARS + v], pl.ds(0, 8), :] + gains[i * VARS + v] for v in range(VARS)]
            for v in range(VARS):
                total[uppers[i * VARS + v], pl.ds(0, 8), :] = sums[v]
        return carry

    lax.fori_loop(0, LOWER // 6, couple, 0, unroll=2)

    def store(group, carry):
        made = []
        for p in range(PAIRS):
            a = total[group * (2 * PAIRS) + p, pl.ds(0, 8), :]
            b = total[group * (2 * PAIRS) + PAIRS + p, pl.ds(0, 8), :]
            made.append(jnp.where(low, a, b) + pltpu.roll(jnp.where(low, b, a), 64, 1))
        for p in range(PAIRS):
            out_ref[group, pl.ds(8 * p, 8), :] = made[p]
        return carry

    lax.fori_loop(0, groups, store, 0, unroll=16)


def unpack_kernel(got_ref, result_ref, out_ref, sem):
    low = lanes_of() < 64
    mask, _ = here()

    def send(r):
        rows = pl.ds(8 * r, 8)
        return pltpu.make_async_copy(out_ref.at[:, rows], result_ref.at[:, rows], sem.at[r])

    for r in range(4):
        for h in range(2):
            for p in range(PAIRS):
                one = got_ref[rank(holder(r, 2 * h) ^ mask), pl.ds(8 * p, 8), :]
                two = got_ref[rank(holder(r, 2 * h + 1) ^ mask), pl.ds(8 * p, 8), :]
                out_ref[p, pl.ds(8 * r, 8), pl.ds(128 * h, 128)] = jnp.where(
                    low, one, pltpu.roll(two, 64, 1)
                )
                out_ref[p + PAIRS, pl.ds(8 * r, 8), pl.ds(128 * h, 128)] = jnp.where(
                    low, pltpu.roll(one, 64, 1), two
                )
        send(r).start()
    for r in range(4):
        send(r).wait()


def vmem():
    return pl.BlockSpec(memory_space=pltpu.VMEM)


def hbm():
    return pl.BlockSpec(memory_space=pltpu.HBM)


def f32(*shape):
    return jax.ShapeDtypeStruct(shape, jnp.float32)


PARAMS = pltpu.CompilerParams(vmem_limit_bytes=32 * 1024 * 1024)


def cost(micros):
    return pl.CostEstimate(flops=0, bytes_accessed=micros * 3000000, transcendentals=0)


def pack(fields, groups):
    return pl.pallas_call(
        pack_kernel,
        out_shape=f32(groups, ROWS, 128),
        in_specs=[vmem()],
        out_specs=hbm(),
        scratch_shapes=[
            pltpu.VMEM((groups, ROWS, 128), jnp.float32),
            pltpu.SemaphoreType.DMA((2, groups)),
        ],
        compiler_params=PARAMS,
        cost_estimate=cost(2),
    )(fields)


def edges(got):
    return pl.pallas_call(
        edge_kernel,
        out_shape=f32(got.shape[0] * PAIRS, 128),
        in_specs=[vmem()],
        out_specs=vmem(),
        compiler_params=PARAMS,
        cost_estimate=cost(1),
    )(got)


def coefs(modes, edge, weights):
    return pl.pallas_call(
        coef_kernel,
        out_shape=f32(modes.shape[0], 16, 128),
        in_specs=[vmem(), vmem(), hbm()],
        out_specs=vmem(),
        compiler_params=PARAMS,
        cost_estimate=cost(1),
    )(modes, edge, weights)


def load(own, got, coef):
    slots = got.shape[0] * 2 * PAIRS
    return pl.pallas_call(
        load_kernel,
        out_shape=(f32(slots, 16, 128), f32(slots, 8, 128)),
        in_specs=[vmem()] * 3,
        out_specs=(vmem(), vmem()),
        compiler_params=PARAMS,
        cost_estimate=cost(4),
    )(own, got, coef)


def mix(places, own, weights, diff, total, edge, coef):
    slots = diff.shape[0]
    return pl.pallas_call(
        mix_kernel,
        out_shape=f32(slots // (2 * PAIRS), BLOCK, 128),
        in_specs=[vmem()] * 7,
        out_specs=vmem(),
        scratch_shapes=[
            pltpu.VMEM((slots, 16, 128), jnp.float32),
            pltpu.VMEM((slots, 16, 128), jnp.float32),
            pltpu.SMEM(places.shape, jnp.int32),
            pltpu.SemaphoreType.DMA,
        ],
        compiler_params=PARAMS,
        cost_estimate=cost(5),
    )(places, own, weights, diff, total, edge, coef)


def unpack(got, shape):
    return pl.pallas_call(
        unpack_kernel,
        out_shape=f32(*shape),
        in_specs=[vmem()],
        out_specs=hbm(),
        scratch_shapes=[pltpu.VMEM(shape, jnp.float32), pltpu.SemaphoreType.DMA((4,))],
        compiler_params=PARAMS,
        cost_estimate=cost(1),
    )(got)


def tables(pair_list, pair_value, assign):
    terms = assign.shape[0]
    numbers = jnp.arange(terms, dtype=jnp.int32)
    row, col, mode = pair_list[:, 0:1], pair_list[:, 1:2], pair_list[:, 2:3]
    slot = jnp.sum(jnp.where(col == assign[None, :], numbers[None, :], 0), axis=1, keepdims=True)
    at = jnp.minimum(row, col) == numbers[None, :]
    kinds = jnp.arange(1 + 3 * VARS, dtype=jnp.int32)[None, :]
    wanted = jnp.where(kinds <= VARS, kinds, (kinds - 1) % VARS + 1)
    side = jnp.where(kinds <= VARS, row <= col, jnp.where(kinds <= 2 * VARS, row > col, row < col))
    value = jnp.where(kinds <= 2 * VARS, pair_value[:, None], slot.astype(jnp.float32))
    value = jnp.where((mode == wanted) & side, value, 0.0)
    found = lax.dot_general(
        at.astype(jnp.float32),
        value,
        (((0,), (0,)), ((), ())),
        precision=lax.Precision.HIGHEST,
        preferred_element_type=jnp.float32,
    )
    coupled = jnp.pad(found[:LOWER, 1 : 1 + 2 * VARS], ((0, 0), (0, 4)))
    uppers = jnp.round(found[:LOWER, 1 + 2 * VARS :]).astype(jnp.int32).reshape(-1)
    weights = jnp.broadcast_to(coupled[:, :, None], coupled.shape + (128,))
    held = assign[:, None] == numbers[None, :]
    own = jnp.sum(jnp.where(held, found[:, 0][None, :], 0.0), axis=1, keepdims=True)
    lowers = jnp.sum(jnp.where(held[:, :LOWER], numbers[:, None], 0), axis=0)
    places = jnp.pad(jnp.concatenate([lowers, uppers]), (0, 1024 - LOWER * (1 + VARS)))
    return places, jnp.broadcast_to(own, (terms, 128)), weights


def shards(fields, modes, pair_list, pair_value, assign):
    groups = lax.axis_size("term")
    count = lax.axis_size("space")
    passes, between = [], []
    for c in range(groups // 4):
        for s in range(count):
            one, two = ((holder(r, c) ^ mask_at(s)) * count + s for r in (1, 2))
            between += [(one, two), (two, one)]
        for s in range(count - 1):
            lower = (holder(0, c) ^ mask_at(s + 1)) * count + s + 1
            upper = (holder(3, c) ^ mask_at(s)) * count + s
            passes += [(lower, upper), (upper, lower)]
    order = sorted(range(groups), key=rank)
    assign = assign.reshape(groups, -1)[jnp.array(order)].reshape(-1)
    sent = pack(fields, groups)
    sent, modes = lax.optimization_barrier((sent, modes))
    got = lax.all_to_all(sent, "term", 0, 0, axis_index_groups=[order], tiled=True)
    places, own, weights = tables(pair_list, pair_value, assign)
    _, place = here()
    edge = jnp.where(row_group(place) == 0, modes[:, 0], modes[:, modes.shape[1] - 1])
    coef = coefs(modes, lax.ppermute(edge, ("term", "space"), passes), weights)
    got, coef, places, own = lax.optimization_barrier((got, coef, places, own))
    beyond = lax.ppermute(edges(got), ("term", "space"), passes + between)
    diff, total = load(own, got, coef)
    mixed = mix(places, own, weights, diff, total, beyond, coef)
    back = lax.all_to_all(mixed, "term", 0, 0, axis_index_groups=[order], tiled=True)
    return unpack(back, fields.shape)


def solution(mesh):
    return jax.shard_map(
        shards,
        mesh=mesh,
        in_specs=(P("term", "space", None), P(None, "space", None), P(), P(), P()),
        out_specs=P("term", "space", None),
        check_vma=False,
    )
```
